512 devices in a mesh: doc: 4 (over y_hi, core), seq: 128 (over z, y_lo, x).
Axes of the slice: x: 4, y: 4 (y_hi: 2, y_lo: 2; y = y_hi * 2 + y_lo), z: 16, core: 2. Of those that a mesh axis runs over, the one named last changes fastest.
Arguments:
- queries: bfloat16 [65536, 512], P(('doc', 'seq')), parts along dimension 0, may hold values from -26 to 26
- key_vectors: bfloat16 [65536, 512], P(('doc', 'seq')), parts along dimension 0, may hold values from -26 to 26
- value_vectors: bfloat16 [65536, 512], P(('doc', 'seq')), parts along dimension 0, may hold values from -6 to 6
- output_grad: bfloat16 [65536, 512], P(('doc', 'seq')), parts along dimension 0, may hold values from -6 to 6
- rand_pick: int32 [1024, 3], P('doc'), parts along dimension 0, may hold values from 0 to 1
- global_ids: int32 [8], P('doc'), parts along dimension 0, may hold values from 0 to 255
Outputs:
- grad_queries: bfloat16 [65536, 512], P(('doc', 'seq')), parts along dimension 0
- grad_keys: bfloat16 [65536, 512], P(('doc', 'seq')), parts along dimension 0
- grad_values: bfloat16 [65536, 512], P(('doc', 'seq')), parts along dimension 0
The draws below stay inside these ranges and needn't reach their ends.
There are 4 independent parts, one for each index of `doc`. The reference program is written for one: setup_inputs(seed, part) draws one part's arguments, and reference() takes and returns one part's arrays. A program takes and returns all parts, laid end to end along the dimension named above; each array names one. Nothing has to cross between parts.
All inputs are finite; a program needn't handle non-finite values.
Results may differ from the reference program's by a relative error of at most 0.012.
Values may be sent and summed in bfloat16 or wider, within the bound.
A program may use at most 64 MiB of HBM per device.

```python
import math
import jax
import jax.numpy as jnp
from jax import lax

D = 512
HEADS = 8
BLOCK = 64
RAND = 3
GLOBAL = 2
RSPAN = 2
TOKENS = 16384
NB = 256


def draw_queries(key, part):
    key = jax.random.fold_in(key, 1)
    drawn = jnp.clip(jax.random.normal(key, (TOKENS, D), jnp.float32), -4.0, 4.0)
    return drawn.astype(jnp.bfloat16)


def draw_key_vectors(key, part):
    key = jax.random.fold_in(key, 2)
    drawn = jnp.clip(jax.random.normal(key, (TOKENS, D), jnp.float32), -4.0, 4.0)
    return drawn.astype(jnp.bfloat16)


def touch_ends(values, rng, low, high):
    place = [jax.random.randint(jax.random.fold_in(rng, axis), (), 0, length) for axis, length in enumerate(values.shape)]
    main_axis = values.shape.index(max(values.shape))
    neighbour = place[:main_axis] + [(place[main_axis] + 1) % values.shape[main_axis]] + place[main_axis + 1:]
    return values.at[tuple(place)].set(low).at[tuple(neighbour)].set(high)


def levels(key, shape, pieces, low, top_value):
    factor_of = 1.0
    for dim, blocks in pieces:
        draws = jax.random.uniform(jax.random.fold_in(jax.random.fold_in(key, 6), dim), (blocks,), jnp.float32, low / len(pieces), top_value / len(pieces))
        factor_of = factor_of * jnp.repeat(jnp.exp(draws), shape[dim] // blocks).reshape((-1,) + (1,) * (len(shape) - 1 - dim))
    return factor_of


def normal_values(own_key, dims, deviation, bound, pieces=(), kind=jnp.bfloat16):
    values = jax.random.normal(own_key, dims, jnp.float32) * deviation
    if len(pieces) > 0:
        values = levels(own_key, dims, pieces, -0.22, 0.18) * values
    return jnp.clip(values, min=-bound, max=bound).astype(kind)


def setup_inputs(seed: int = 0, part: int = 0) -> dict:
    keys = jax.random.split(jax.random.key(seed), 7)
    part_splits = jax.random.split(jax.random.fold_in(keys[6], part), 7)
    queries = draw_queries(jax.random.fold_in(jax.random.fold_in(keys[6], part), 71), part)
    key_vectors = draw_key_vectors(jax.random.fold_in(jax.random.fold_in(keys[6], part), 71), part)
    value_vectors = normal_values(part_splits[2], (TOKENS, D), 1.0, 6.0, ((0, 128),))
    output_grad = normal_values(part_splits[3], (TOKENS, D), 1.0, 6.0, ((0, 128),))
    rand_pick = touch_ends(jax.random.randint(part_splits[4], (NB, RAND), 0, RSPAN), jax.random.fold_in(part_splits[4], 1), 0, RSPAN - 1).astype(jnp.int32)
    global_ids = jax.random.randint(part_splits[5], (GLOBAL,), 0, NB).astype(jnp.int32)
    return dict(queries=queries, key_vectors=key_vectors, value_vectors=value_vectors, output_grad=output_grad, rand_pick=rand_pick, global_ids=global_ids)


def reference(queries, key_vectors, value_vectors, output_grad, rand_pick, global_ids):
    num_blocks = TOKENS // BLOCK
    head_size = D // HEADS
    scale = 1.0 / math.sqrt(head_size)
    entries = 3 + GLOBAL + RAND
    query_blocks = queries.reshape(num_blocks, BLOCK, HEADS, head_size)
    grad_blocks = output_grad.reshape(num_blocks, BLOCK, HEADS, head_size)
    pair_blocks = jnp.concatenate([key_vectors, value_vectors], axis=1).reshape(num_blocks, BLOCK, 2 * D)
    segment = jnp.arange(entries * BLOCK, dtype=jnp.int32) // BLOCK

    def visit(totals, block_idx):
        chosen = [jnp.maximum(block_idx - 1, 0), block_idx, jnp.minimum(block_idx + 1, num_blocks - 1)]
        chosen += [global_ids[slot_idx] for slot_idx in range(GLOBAL)]
        chosen += [(block_idx - (slot_idx + 1) * num_blocks // 4 - rand_pick[block_idx, slot_idx]) % num_blocks for slot_idx in range(RAND)]
        listed = jnp.stack([item.astype(jnp.int32) for item in chosen]).astype(jnp.int32)
        gathered = jnp.take(pair_blocks, listed, axis=0).reshape(entries * BLOCK, 2 * D)
        key_part = gathered[:, :D].reshape(-1, HEADS, head_size).astype(jnp.float32)
        value_part = gathered[:, D:].reshape(-1, HEADS, head_size).astype(jnp.float32)
        query_part = lax.dynamic_index_in_dim(query_blocks, block_idx, 0, keepdims=False).astype(jnp.float32)
        grad_part = lax.dynamic_index_in_dim(grad_blocks, block_idx, 0, keepdims=False).astype(jnp.float32)
        valid = ((segment != 0) | (block_idx > 0)) & ((segment != 2) | (block_idx < num_blocks - 1))
        scores = jnp.einsum('qhe,khe->hqk', query_part, key_part) * scale
        scores = jnp.where(valid[None, None, :], scores, -1e+30)
        row_max = lax.optimization_barrier(jnp.max(scores, axis=-1, keepdims=True))
        expo = jnp.exp(scores - row_max)
        row_total = lax.optimization_barrier(jnp.sum(expo, axis=-1, keepdims=True))
        probs = expo / row_total
        probs_half = lax.optimization_barrier(probs.astype(jnp.bfloat16)).astype(jnp.float32)
        attended = jnp.einsum('hqk,khe->qhe', probs_half, value_part)
        row_dot = lax.optimization_barrier(jnp.sum(grad_part * attended, axis=-1)).T
        grad_probs = jnp.einsum('qhe,khe->hqk', grad_part, value_part)
        grad_scores = probs * (grad_probs - row_dot[:, :, None])
        grad_half = lax.optimization_barrier(grad_scores.astype(jnp.bfloat16)).astype(jnp.float32)
        grad_query = jnp.einsum('hqk,khe->qhe', grad_half, key_part) * scale
        grad_key = jnp.einsum('hqk,qhe->khe', grad_half, query_part) * scale
        grad_value = jnp.einsum('hqk,qhe->khe', probs_half, grad_part)
        update = jnp.concatenate([grad_key.reshape(-1, D), grad_value.reshape(-1, D)], axis=1)
        totals = totals.at[listed].add(update.reshape(entries, BLOCK, 2 * D))
        return (totals, grad_query.reshape(BLOCK, D).astype(jnp.bfloat16))
    start = jnp.zeros((num_blocks, BLOCK, 2 * D), jnp.float32)
    totals, grad_query = lax.scan(visit, start, jnp.arange(num_blocks, dtype=jnp.int32))
    flat = totals.reshape(TOKENS, 2 * D)
    return (grad_query.reshape(TOKENS, D), flat[:, :D].astype(jnp.bfloat16), flat[:, D:].astype(jnp.bfloat16))
```

```python
import functools

import jax
import jax.numpy as jnp
from jax import lax
from jax.experimental import pallas as pl
from jax.experimental.pallas import tpu as pltpu
from jax.sharding import PartitionSpec as P

MESH = pl.DeviceIdType.MESH
BLOCK = 64
RAND = 3
GLOBAL = 2
PARTS = 4
PLANE = 8
LAYERS = 4
GROUPS = PLANE * LAYERS
SEQ = PARTS * GROUPS
W = 128
HALF = 64
BF = jnp.bfloat16
F32 = jnp.float32


def kernel(
    q_hbm, k_hbm, v_hbm, do_hbm, pick_ref, gid_ref,
    dq_out, dk_out, dv_out,
    q_all, do_all, kv_own, kv_left, kv_right,
    cand, g1, g2, kv_glob,
    acc_own, acc_left, acc_right, acc_glob,
    edge_out, edge_in, h1, h2, tot_glob,
    dq_stage, dk_stage, dv_stage,
    in_send, in_recv, edge_send, edge_recv, g_send, g_recv,
    dq_send, dq_recv, dkv_send, dkv_recv,
):
    me = lax.axis_index("seq")
    part = lax.div(me, GROUPS)
    group = lax.rem(me, GROUPS)
    layer = lax.div(group, PLANE)
    spot = lax.rem(group, PLANE)

    def mate(quarter):
        return {"seq": quarter * GROUPS + group}

    def in_plane(other):
        return {"seq": part * GROUPS + layer * PLANE + other}

    def in_layer(other):
        return {"seq": part * GROUPS + other * PLANE + spot}

    right = {"seq": part * GROUPS + lax.rem(group + 1, GROUPS)}
    left = {"seq": part * GROUPS + lax.rem(group + GROUPS - 1, GROUPS)}

    barrier = pltpu.get_barrier_semaphore()

    def greet(where):
        pl.semaphore_signal(barrier, inc=1, device_id=where, device_id_type=MESH)

    for j in range(1, PARTS):
        greet(mate(lax.rem(part + j, PARTS)))
    greet(left)
    greet(right)
    for o in range(1, PLANE):
        greet(in_plane(lax.rem(spot + o, PLANE)))
    for o in range(1, LAYERS):
        greet(in_layer(lax.rem(layer + o, LAYERS)))
    pl.semaphore_wait(barrier, PARTS - 1 + 2 + PLANE - 1 + LAYERS - 1)

    def remote(src, dst, send, recv, where):
        return pltpu.make_async_remote_copy(
            src_ref=src, dst_ref=dst, send_sem=send, recv_sem=recv, device_id=where,
            device_id_type=MESH,
        )

    two = 2 * W

    def cols(quarter):
        return pl.ds(pl.multiple_of(quarter * W, W), W)

    arrays = (
        (k_hbm, lambda s: kv_own.at[s, :, 0:W]),
        (v_hbm, lambda s: kv_own.at[s, :, W : 2 * W]),
        (q_hbm, lambda s: q_all.at[s]),
        (do_hbm, lambda s: do_all.at[s]),
    )

    def incoming(n, j):
        hbm, place = arrays[n]
        to = lax.rem(part + j, PARTS)
        return remote(
            hbm.at[:, cols(to)], place(part), in_send.at[n, j], in_recv.at[n, j], mate(to)
        )

    def own_copy(n):
        hbm, place = arrays[n]
        return pltpu.make_async_copy(hbm.at[:, cols(part)], place(part), in_recv.at[n, 0])

    for n in range(4):
        for j in (2, 1, 3):
            incoming(n, j).start()
        own_copy(n).start()

    acc_own[...] = jnp.zeros_like(acc_own)
    acc_left[...] = jnp.zeros_like(acc_left)
    acc_right[...] = jnp.zeros_like(acc_right)
    acc_glob[...] = jnp.zeros_like(acc_glob)

    for n in range(2):
        own_copy(n).wait()
        for j in (1, 3, 2):
            incoming(n, j).wait_recv()

    to_right = remote(
        kv_own.at[:, BLOCK : 2 * BLOCK, :], kv_left, edge_send.at[0], edge_recv.at[0], right
    )
    to_left = remote(
        kv_own.at[:, 0:BLOCK, :], kv_right, edge_send.at[1], edge_recv.at[1], left
    )
    to_right.start()
    to_left.start()

    def choose(code, options):
        code = jnp.full((1, two), code, jnp.int32)
        total = None
        for n, option in enumerate(options):
            option = option.astype(F32)
            term = jnp.where(code == n, option, jnp.zeros_like(option))
            total = term if total is None else total + term
        return total.astype(BF)

    for m in range(GLOBAL):
        gid = gid_ref[m]
        cand[m * BLOCK : (m + 1) * BLOCK, :] = choose(
            lax.div(gid, 2 * GROUPS) * 2 + lax.rem(gid, 2),
            [kv_own[s, b * BLOCK : (b + 1) * BLOCK, :] for s in range(PARTS) for b in range(2)],
        )

    def rows(t):
        return pl.ds(pl.multiple_of(t * 16, 16), 16)

    my_gid = gid_ref[lax.div(spot, PLANE // GLOBAL)]
    gid_spot = lax.rem(lax.div(my_gid, 2), PLANE)
    gid_layer = lax.rem(lax.div(my_gid, 2 * PLANE), LAYERS)

    def scatter_plane(source, slots, base):
        def copy(o):
            to = lax.rem(spot + o, PLANE)
            return remote(
                source.at[rows(to)], slots.at[spot], g_send.at[base, o], g_recv.at[base, o],
                in_plane(to),
            )
        return copy

    def spread_layers(slots, base):
        def copy(o):
            to = lax.rem(layer + o, LAYERS)
            return remote(
                slots.at[layer], slots.at[layer], g_send.at[base, o], g_recv.at[base, o],
                in_layer(to),
            )
        return copy

    def gather_plane(whole, base):
        def copy(o):
            to = lax.rem(spot + o, PLANE)
            return remote(
                whole.at[rows(spot)], whole.at[rows(spot)], g_send.at[base, o],
                g_recv.at[base, o], in_plane(to),
            )
        return copy

    def start_all(copy, count):
        def step(o, _):
            copy(o).start()
            return 0
        lax.fori_loop(1, count, step, 0)

    def wait_all(copy, count):
        def step(o, _):
            copy(o).wait()
            return 0
        lax.fori_loop(1, count, step, 0)

    c1 = scatter_plane(cand, g1, 0)
    start_all(c1, PLANE)
    g1[spot] = cand[rows(spot), :]
    wait_all(c1, PLANE)
    g2[layer] = choose(gid_spot, [g1[t] for t in range(PLANE)])
    c2 = spread_layers(g2, 1)
    start_all(c2, LAYERS)
    wait_all(c2, LAYERS)
    kv_glob[rows(spot), :] = choose(gid_layer, [g2[t] for t in range(LAYERS)])
    c3 = gather_plane(kv_glob, 2)
    start_all(c3, PLANE)
    wait_all(c3, PLANE)

    to_right.wait()
    to_left.wait()

    first_group = (group == 0).astype(jnp.int32)
    last_group = (group == GROUPS - 1).astype(jnp.int32)
    low = lax.broadcasted_iota(jnp.int32, (BLOCK, W), 1) < HALF

    def two_heads(x):
        x = x.astype(F32)
        zero = jnp.zeros_like(x)
        return jnp.concatenate([jnp.where(low, x, zero), jnp.where(low, zero, x)], axis=0)

    def dot(a, b, dims):
        return lax.dot_general(a, b, (dims, ((), ())), preferred_element_type=F32)

    def outgoing_dq(j):
        to = lax.rem(part + j, PARTS)
        return remote(
            dq_stage.at[to], dq_out.at[:, cols(part)], dq_send.at[j], dq_recv.at[j], mate(to)
        )

    def own_dq():
        return pltpu.make_async_copy(dq_stage.at[part], dq_out.at[:, cols(part)], dq_recv.at[0])

    def visit(t, _):
        j = t + t // 2 - 2 * (t // 3)
        here = lax.rem(part + PARTS - j, PARTS)
        for n in (2, 3):
            @pl.when(j == 0)
            def _():
                own_copy(n).wait()

            @pl.when(j != 0)
            def _():
                incoming(n, j).wait_recv()

        at_left = lax.rem(here + (PARTS - 1) * first_group, PARTS)
        at_right = lax.rem(here + last_group, PARTS)
        for b in range(2):
            number = here * (2 * GROUPS) + 2 * group + b
            own0 = (kv_own, here, 0, acc_own)
            own1 = (kv_own, here, BLOCK, acc_own)
            window = [
                (kv_left, at_left, 0, acc_left) if b == 0 else own0,
                own0 if b == 0 else own1,
                own1 if b == 0 else (kv_right, at_right, 0, acc_right),
            ]
            def load(entry):
                ref, s, start, _ = entry
                return ref[s, start : start + BLOCK, :]

            def add(entry, value):
                _, s, start, acc = entry
                acc[s, start : start + BLOCK, :] += value

            choices = []
            taken = []
            pieces = [load(e) for e in window]
            pieces.append(kv_glob[...])
            for s in range(RAND):
                far = lax.rem(here + PARTS - (s + 1), PARTS)
                far_left = lax.rem(far + (PARTS - 1) * first_group, PARTS)
                pick = jnp.full((1, two), pick_ref[s, number].astype(F32)).astype(BF)
                near_entry = (kv_own, far, b * BLOCK, acc_own)
                far_entry = (kv_left, far_left, 0, acc_left) if b == 0 else (kv_own, far, 0, acc_own)
                choices.append((near_entry, far_entry))
                taken.append(pick)
                pieces.append(load(near_entry) * (1 - pick) + load(far_entry) * pick)
            listed = jnp.concatenate(pieces, axis=0)
            keys = listed[:, 0:W]
            values = listed[:, W : 2 * W]
            q2 = (two_heads(q_all[here, b * BLOCK : (b + 1) * BLOCK, :]) * 0.125).astype(BF)
            do2 = two_heads(do_all[here, b * BLOCK : (b + 1) * BLOCK, :]).astype(BF)
            scores = dot(keys, q2, ((1,), (1,)))
            if b == 0:
                masked = jnp.where(number == 0, -1e30, scores[:BLOCK])
                scores = jnp.concatenate([masked, scores[BLOCK:]], axis=0)
            else:
                masked = jnp.where(number == 2 * SEQ - 1, -1e30, scores[2 * BLOCK : 3 * BLOCK])
                scores = jnp.concatenate(
                    [scores[: 2 * BLOCK], masked, scores[3 * BLOCK :]], axis=0
                )
            row_max = jnp.max(scores, axis=0, keepdims=True)
            expo = jnp.exp(scores - row_max)
            row_total = jnp.sum(expo, axis=0, keepdims=True)
            probs = expo * (1.0 / row_total)
            probs_half = probs.astype(BF)
            grad_probs = dot(values, do2, ((1,), (1,)))
            row_dot = jnp.sum(probs_half.astype(F32) * grad_probs, axis=0, keepdims=True)
            grad_half = (probs * (grad_probs - row_dot)).astype(BF)
            back = dot(grad_half, keys, ((0,), (0,)))
            dq_stage[here, b * BLOCK : (b + 1) * BLOCK, :] = (
                jnp.where(low, back[:BLOCK], back[BLOCK:]) * 0.125
            ).astype(BF)
            grads = jnp.concatenate(
                [dot(grad_half, q2, ((1,), (0,))), dot(probs_half, do2, ((1,), (0,)))], axis=1
            )
            for n, entry in enumerate(window):
                add(entry, grads[n * BLOCK : (n + 1) * BLOCK])
            acc_glob[...] += grads[3 * BLOCK : (3 + GLOBAL) * BLOCK]
            for s in range(RAND):
                part_grad = grads[(3 + GLOBAL + s) * BLOCK : (4 + GLOBAL + s) * BLOCK]
                near_entry, far_entry = choices[s]
                far_grad = part_grad * taken[s].astype(F32)
                add(near_entry, part_grad - far_grad)
                add(far_entry, far_grad)

        @pl.when(j == 0)
        def _():
            own_dq().start()

        @pl.when(j != 0)
        def _():
            outgoing_dq(PARTS - j).start()

        return 0

    lax.fori_loop(0, PARTS, visit, 0)

    c4 = scatter_plane(acc_glob, h1, 3)
    start_all(c4, PLANE)
    edge_out[0] = acc_left[...].astype(BF)
    edge_out[1] = acc_right[...].astype(BF)
    back_left = remote(edge_out.at[0], edge_in.at[0], edge_send.at[2], edge_recv.at[2], left)
    back_right = remote(edge_out.at[1], edge_in.at[1], edge_send.at[3], edge_recv.at[3], right)
    back_left.start()
    back_right.start()
    h1[spot] = acc_glob[rows(spot), :]
    wait_all(c4, PLANE)
    h2[layer] = jnp.sum(h1[...], axis=0)
    c5 = spread_layers(h2, 4)
    start_all(c5, LAYERS)
    wait_all(c5, LAYERS)
    tot_glob[rows(spot), :] = jnp.sum(h2[...], axis=0)
    c6 = gather_plane(tot_glob, 5)
    start_all(c6, PLANE)

    back_left.wait()
    back_right.wait()
    acc_own[:, BLOCK : 2 * BLOCK, :] += edge_in[0].astype(F32)
    acc_own[:, 0:BLOCK, :] += edge_in[1].astype(F32)
    wait_all(c6, PLANE)

    def outgoing(stage, out, n, j):
        to = lax.rem(part + j, PARTS)
        return remote(
            stage.at[to], out.at[:, cols(part)], dkv_send.at[n, j], dkv_recv.at[n, j], mate(to)
        )

    def own_out(stage, out, n):
        return pltpu.make_async_copy(stage.at[part], out.at[:, cols(part)], dkv_recv.at[n, 0])

    results = ((dk_stage, dk_out), (dv_stage, dv_out))
    for j in (2, 1, 3, 0):
        there = lax.rem(part + j, PARTS)
        for b in range(2):
            number = there * (2 * GROUPS) + 2 * group + b
            total = acc_own[there, b * BLOCK : (b + 1) * BLOCK, :]
            for m in range(GLOBAL):
                extra = tot_glob[m * BLOCK : (m + 1) * BLOCK, :]
                named = jnp.full((1, two), gid_ref[m], jnp.int32) == number
                total = total + jnp.where(named, extra, jnp.zeros_like(extra))
            dk_stage[there, b * BLOCK : (b + 1) * BLOCK, :] = total[:, 0:W].astype(BF)
            dv_stage[there, b * BLOCK : (b + 1) * BLOCK, :] = total[:, W : 2 * W].astype(BF)
        for n, (stage, out) in enumerate(results):
            if j == 0:
                own_out(stage, out, n).start()
            else:
                outgoing(stage, out, n, j).start()

    for n in range(4):
        for j in range(1, PARTS):
            incoming(n, j).wait_send()
    own_dq().wait()
    for j in range(1, PARTS):
        outgoing_dq(j).wait()
    for n, (stage, out) in enumerate(results):
        own_out(stage, out, n).wait()
        for j in range(1, PARTS):
            outgoing(stage, out, n, j).wait()


def on_device(queries, key_vectors, value_vectors, output_grad, rand_pick, global_ids):
    rows, width = queries.shape
    out = jax.ShapeDtypeStruct((rows, width), BF)
    anywhere = pl.BlockSpec(memory_space=pl.ANY)
    small = pl.BlockSpec(memory_space=pltpu.SMEM)
    two = 2 * W
    scratch = [
        pltpu.VMEM((PARTS, 2 * BLOCK, W), BF),
        pltpu.VMEM((PARTS, 2 * BLOCK, W), BF),
        pltpu.VMEM((PARTS, 2 * BLOCK, two), BF),
        pltpu.VMEM((PARTS, BLOCK, two), BF),
        pltpu.VMEM((PARTS, BLOCK, two), BF),
        pltpu.VMEM((GLOBAL * BLOCK, two), BF),
        pltpu.VMEM((PLANE, 16, two), BF),
        pltpu.VMEM((LAYERS, 16, two), BF),
        pltpu.VMEM((GLOBAL * BLOCK, two), BF),
        pltpu.VMEM((PARTS, 2 * BLOCK, two), F32),
        pltpu.VMEM((PARTS, BLOCK, two), F32),
        pltpu.VMEM((PARTS, BLOCK, two), F32),
        pltpu.VMEM((GLOBAL * BLOCK, two), F32),
        pltpu.VMEM((2, PARTS, BLOCK, two), BF),
        pltpu.VMEM((2, PARTS, BLOCK, two), BF),
        pltpu.VMEM((PLANE, 16, two), F32),
        pltpu.VMEM((LAYERS, 16, two), F32),
        pltpu.VMEM((GLOBAL * BLOCK, two), F32),
        pltpu.VMEM((PARTS, 2 * BLOCK, W), BF),
        pltpu.VMEM((PARTS, 2 * BLOCK, W), BF),
        pltpu.VMEM((PARTS, 2 * BLOCK, W), BF),
        pltpu.SemaphoreType.DMA((4, PARTS)),
        pltpu.SemaphoreType.DMA((4, PARTS)),
        pltpu.SemaphoreType.DMA((4,)),
        pltpu.SemaphoreType.DMA((4,)),
        pltpu.SemaphoreType.DMA((6, PLANE)),
        pltpu.SemaphoreType.DMA((6, PLANE)),
        pltpu.SemaphoreType.DMA((PARTS,)),
        pltpu.SemaphoreType.DMA((PARTS,)),
        pltpu.SemaphoreType.DMA((2, PARTS)),
        pltpu.SemaphoreType.DMA((2, PARTS)),
    ]
    return pl.pallas_call(
        kernel,
        out_shape=(out, out, out),
        in_specs=[anywhere] * 4 + [small] * 2,
        out_specs=(anywhere,) * 3,
        scratch_shapes=scratch,
        compiler_params=pltpu.CompilerParams(
            collective_id=1, has_side_effects=True, vmem_limit_bytes=32 * 1024 * 1024
        ),
        name="sparse_attention_grads",
    )(queries, key_vectors, value_vectors, output_grad, rand_pick.T, global_ids)


def solution(mesh):
    spec = P(("doc", "seq"), None)
    return jax.shard_map(
        on_device,
        mesh=mesh,
        in_specs=(spec, spec, spec, spec, P("doc", None), P("doc")),
        out_specs=(spec, spec, spec),
        check_vma=False,
    )
```

```python
import functools

import jax
import jax.numpy as jnp
from jax import lax
from jax.experimental import pallas as pl
from jax.experimental.pallas import tpu as pltpu
from jax.sharding import PartitionSpec as P

MESH = pl.DeviceIdType.MESH
BLOCK = 64
RAND = 3
GLOBAL = 2
PARTS = 4
PLANE = 8
LAYERS = 4
GROUPS = PLANE * LAYERS
SEQ = PARTS * GROUPS
W = 128
HALF = 64
FULL = PARTS * W
BF = jnp.bfloat16
F32 = jnp.float32


def kernel(
    q_hbm, k_hbm, v_hbm, do_hbm, pick_ref, gid_ref,
    dq_out, dk_out, dv_out,
    q_all, do_all, kv_own, kv_left, kv_right,
    kv_raw, cand, g1, g2_out, g2, g3, kv_glob,
    acc_own, acc_left, acc_right, acc_glob,
    edge_out, edge_in, h1_out, h1, h2, h3,
    dq_stage, dk_stage, dv_stage,
    raw_sem, in_send, in_recv, edge_send, edge_recv, g_send, g_recv,
    dq_send, dq_recv, dkv_send, dkv_recv,
):
    me = lax.axis_index("seq")
    part = lax.div(me, GROUPS)
    group = lax.rem(me, GROUPS)
    layer = lax.div(group, PLANE)
    spot = lax.rem(group, PLANE)

    def mate(quarter):
        return {"seq": quarter * GROUPS + group}

    def in_plane(other):
        return {"seq": part * GROUPS + layer * PLANE + other}

    def in_layer(other):
        return {"seq": part * GROUPS + other * PLANE + spot}

    right = {"seq": part * GROUPS + lax.rem(group + 1, GROUPS)}
    left = {"seq": part * GROUPS + lax.rem(group + GROUPS - 1, GROUPS)}

    barrier = pltpu.get_barrier_semaphore()

    def greet(where):
        pl.semaphore_signal(barrier, inc=1, device_id=where, device_id_type=MESH)

    for j in range(1, PARTS):
        greet(mate(lax.rem(part + j, PARTS)))
    greet(left)
    greet(right)
    for o in range(1, PLANE):
        greet(in_plane(lax.rem(spot + o, PLANE)))
    for o in range(1, LAYERS):
        greet(in_layer(lax.rem(layer + o, LAYERS)))
    def remote(src, dst, send, recv, where):
        return pltpu.make_async_remote_copy(
            src_ref=src, dst_ref=dst, send_sem=send, recv_sem=recv, device_id=where,
            device_id_type=MESH,
        )

    two = 2 * W

    def cols(quarter):
        return pl.ds(pl.multiple_of(quarter * W, W), W)

    arrays = (
        (k_hbm, lambda s: kv_own.at[s, :, 0:W]),
        (v_hbm, lambda s: kv_own.at[s, :, W : 2 * W]),
        (q_hbm, lambda s: q_all.at[s]),
        (do_hbm, lambda s: do_all.at[s]),
    )

    def incoming(n, j):
        hbm, place = arrays[n]
        to = lax.rem(part + j, PARTS)
        return remote(
            hbm.at[:, cols(to)], place(part), in_send.at[n, j], in_recv.at[n, j], mate(to)
        )

    def own_copy(n):
        hbm, place = arrays[n]
        return pltpu.make_async_copy(hbm.at[:, cols(part)], place(part), in_recv.at[n, 0])

    def raw_copy(n):
        return pltpu.make_async_copy((k_hbm, v_hbm)[n], kv_raw.at[n], raw_sem.at[n])

    for n in range(2):
        raw_copy(n).start()
    for n in range(4):
        own_copy(n).start()

    acc_own[...] = jnp.zeros_like(acc_own)
    acc_left[...] = jnp.zeros_like(acc_left)
    acc_right[...] = jnp.zeros_like(acc_right)
    acc_glob[...] = jnp.zeros_like(acc_glob)

    def choose(code, options):
        code = jnp.full((1, options[0].shape[-1]), code, jnp.int32)
        total = None
        for n, option in enumerate(options):
            option = option.astype(F32)
            term = jnp.where(code == n, option, jnp.zeros_like(option))
            total = term if total is None else total + term
        return total.astype(BF)

    def rows(t):
        return pl.ds(pl.multiple_of(t * 16, 16), 16)

    for n in range(2):
        raw_copy(n).wait()
    for t in range(PLANE):
        odd = lax.rem(gid_ref[t // (PLANE // GLOBAL)], 2)
        start = (t % (PLANE // GLOBAL)) * 16
        for n in range(2):
            cand[t, :, n * FULL : (n + 1) * FULL] = choose(
                odd, [kv_raw[n, b * BLOCK + start : b * BLOCK + start + 16, :] for b in range(2)]
            )

    my_gid = gid_ref[lax.div(spot, PLANE // GLOBAL)]
    gid_spot = lax.rem(lax.div(my_gid, 2), PLANE)
    gid_layer = lax.rem(lax.div(my_gid, 2 * PLANE), LAYERS)
    gid_part = lax.div(my_gid, 2 * GROUPS)

    def around(base, count, here, where, source, place):
        def copy(o):
            to = lax.rem(here + o, count)
            return remote(
                source(to), place(here), g_send.at[base, o], g_recv.at[base, o], where(to)
            )
        return copy

    finish = []

    def start_all(copy, count):
        for o in range(1, count):
            copy(o).start()

    def wait_all(copy, count):
        for o in range(1, count):
            copy(o).wait_recv()
        finish.append((copy, count))

    c1 = around(0, PLANE, spot, in_plane, lambda to: cand.at[to], lambda i: g1.at[i])
    c2 = around(1, PARTS, part, mate, lambda to: g2_out.at[to], lambda i: g2.at[i])
    c3 = around(2, LAYERS, layer, in_layer, lambda to: g3.at[layer], lambda i: g3.at[i])
    c4 = around(
        3, PLANE, spot, in_plane, lambda to: kv_glob.at[rows(spot)], lambda i: kv_glob.at[rows(i)]
    )

    to_right = remote(
        kv_own.at[:, BLOCK : 2 * BLOCK, :], kv_left, edge_send.at[0], edge_recv.at[0], right
    )
    to_left = remote(
        kv_own.at[:, 0:BLOCK, :], kv_right, edge_send.at[1], edge_recv.at[1], left
    )

    pl.semaphore_wait(barrier, PARTS - 1 + 2 + PLANE - 1 + LAYERS - 1)


    def send(n, j):
        incoming(n, j).start()

    start_all(c1, PLANE)
    for j in (2, 1, 3):
        send(0, j)
    g1[spot] = cand[spot]
    wait_all(c1, PLANE)
    piece = choose(gid_spot, [g1[t] for t in range(PLANE)])
    for h in range(PARTS):
        g2_out[h, :, 0:W] = piece[:, h * W : (h + 1) * W]
        g2_out[h, :, W:two] = piece[:, FULL + h * W : FULL + (h + 1) * W]
    start_all(c2, PARTS)
    for j in (2, 1, 3):
        send(1, j)
    for j in (2, 1):
        for n in (2, 3):
            send(n, j)
    g2[part] = g2_out[part]
    wait_all(c2, PARTS)
    g3[layer] = choose(gid_part, [g2[t] for t in range(PARTS)])
    start_all(c3, LAYERS)

    for n in range(2):
        own_copy(n).wait()
        for j in (1, 3, 2):
            incoming(n, j).wait_recv()
    to_right.start()
    to_left.start()
    for j in (3,):
        for n in (2, 3):
            send(n, j)
    wait_all(c3, LAYERS)
    kv_glob[rows(spot), :] = choose(gid_layer, [g3[t] for t in range(LAYERS)])
    start_all(c4, PLANE)
    wait_all(c4, PLANE)
    to_right.wait()
    to_left.wait()

    first_group = (group == 0).astype(jnp.int32)
    last_group = (group == GROUPS - 1).astype(jnp.int32)
    low = lax.broadcasted_iota(jnp.int32, (BLOCK, W), 1) < HALF

    def two_heads(x):
        x = x.astype(F32)
        zero = jnp.zeros_like(x)
        return jnp.concatenate([jnp.where(low, x, zero), jnp.where(low, zero, x)], axis=0)

    def dot(a, b, dims):
        return lax.dot_general(a, b, (dims, ((), ())), preferred_element_type=F32)

    def outgoing_dq(j):
        to = lax.rem(part + j, PARTS)
        return remote(
            dq_stage.at[to], dq_out.at[:, cols(part)], dq_send.at[j], dq_recv.at[j], mate(to)
        )

    def own_dq():
        return pltpu.make_async_copy(dq_stage.at[part], dq_out.at[:, cols(part)], dq_recv.at[0])

    def visit(t, _):
        j = t + (t == 1).astype(jnp.int32) - (t == 2).astype(jnp.int32)
        here = lax.rem(part + PARTS - j, PARTS)
        for n in (2, 3):
            @pl.when(j == 0)
            def _():
                own_copy(n).wait()

            @pl.when(j != 0)
            def _():
                incoming(n, j).wait_recv()

        at_left = lax.rem(here + (PARTS - 1) * first_group, PARTS)
        at_right = lax.rem(here + last_group, PARTS)
        for b in range(2):
            number = here * (2 * GROUPS) + 2 * group + b
            own0 = (kv_own, here, 0, acc_own)
            own1 = (kv_own, here, BLOCK, acc_own)
            window = [
                (kv_left, at_left, 0, acc_left) if b == 0 else own0,
                own0 if b == 0 else own1,
                own1 if b == 0 else (kv_right, at_right, 0, acc_right),
            ]
            def load(entry):
                ref, s, start, _ = entry
                return ref[s, start : start + BLOCK, :]

            def add(entry, value):
                _, s, start, acc = entry
                acc[s, start : start + BLOCK, :] += value

            choices = []
            taken = []
            pieces = [load(e) for e in window]
            pieces.append(kv_glob[...])
            for s in range(RAND):
                far = lax.rem(here + PARTS - (s + 1), PARTS)
                far_left = lax.rem(far + (PARTS - 1) * first_group, PARTS)
                pick = jnp.full((1, two), pick_ref[s, number].astype(F32)).astype(BF)
                near_entry = (kv_own, far, b * BLOCK, acc_own)
                far_entry = (kv_left, far_left, 0, acc_left) if b == 0 else (kv_own, far, 0, acc_own)
                choices.append((near_entry, far_entry))
                taken.append(pick)
                pieces.append(load(near_entry) * (1 - pick) + load(far_entry) * pick)
            listed = jnp.concatenate(pieces, axis=0)
            keys = listed[:, 0:W]
            values = listed[:, W : 2 * W]
            q2 = (two_heads(q_all[here, b * BLOCK : (b + 1) * BLOCK, :]) * 0.125).astype(BF)
            do2 = two_heads(do_all[here, b * BLOCK : (b + 1) * BLOCK, :]).astype(BF)
            scores = dot(keys, q2, ((1,), (1,)))
            if b == 0:
                masked = jnp.where(number == 0, -1e30, scores[:BLOCK])
                scores = jnp.concatenate([masked, scores[BLOCK:]], axis=0)
            else:
                masked = jnp.where(number == 2 * SEQ - 1, -1e30, scores[2 * BLOCK : 3 * BLOCK])
                scores = jnp.concatenate(
                    [scores[: 2 * BLOCK], masked, scores[3 * BLOCK :]], axis=0
                )
            row_max = jnp.max(scores, axis=0, keepdims=True)
            expo = jnp.exp(scores - row_max)
            row_total = jnp.sum(expo, axis=0, keepdims=True)
            probs = expo * (1.0 / row_total)
            probs_half = probs.astype(BF)
            grad_probs = dot(values, do2, ((1,), (1,)))
            row_dot = jnp.sum(probs_half.astype(F32) * grad_probs, axis=0, keepdims=True)
            grad_half = (probs * (grad_probs - row_dot)).astype(BF)
            back = dot(grad_half, keys, ((0,), (0,)))
            dq_stage[here, b * BLOCK : (b + 1) * BLOCK, :] = (
                jnp.where(low, back[:BLOCK], back[BLOCK:]) * 0.125
            ).astype(BF)
            grads = jnp.concatenate(
                [dot(grad_half, q2, ((1,), (0,))), dot(probs_half, do2, ((1,), (0,)))], axis=1
            )
            for n, entry in enumerate(window):
                add(entry, grads[n * BLOCK : (n + 1) * BLOCK])
            acc_glob[...] += grads[3 * BLOCK : (3 + GLOBAL) * BLOCK]
            for s in range(RAND):
                part_grad = grads[(3 + GLOBAL + s) * BLOCK : (4 + GLOBAL + s) * BLOCK]
                near_entry, far_entry = choices[s]
                far_grad = part_grad * taken[s].astype(F32)
                add(near_entry, part_grad - far_grad)
                add(far_entry, far_grad)

        return 0

    lax.fori_loop(0, PARTS, visit, 0)

    d1 = around(4, PLANE, spot, in_plane, lambda to: h1_out.at[to], lambda i: h1.at[i])
    d2 = around(5, LAYERS, layer, in_layer, lambda to: h2.at[layer], lambda i: h2.at[i])
    d3 = around(6, PLANE, spot, in_plane, lambda to: h3.at[spot], lambda i: h3.at[i])

    for t in range(PLANE):
        h1_out[t] = acc_glob[t * 16 : (t + 1) * 16, :].astype(BF)
    start_all(d1, PLANE)
    edge_out[0] = acc_left[...].astype(BF)
    edge_out[1] = acc_right[...].astype(BF)
    back_left = remote(edge_out.at[0], edge_in.at[0], edge_send.at[2], edge_recv.at[2], left)
    back_right = remote(edge_out.at[1], edge_in.at[1], edge_send.at[3], edge_recv.at[3], right)
    back_left.start()
    back_right.start()
    own_dq().start()
    outgoing_dq(2).start()
    h1[spot] = h1_out[spot]
    wait_all(d1, PLANE)
    h2[layer] = jnp.sum(h1[...].astype(F32), axis=0).astype(BF)
    start_all(d2, LAYERS)
    outgoing_dq(1).start()
    outgoing_dq(3).start()
    back_left.wait()
    back_right.wait()
    for b in range(2):
        acc_own[:, b * BLOCK : (b + 1) * BLOCK, :] += edge_in[1 - b].astype(F32)
    wait_all(d2, LAYERS)
    h3[spot] = jnp.sum(h2[...].astype(F32), axis=0).astype(BF)
    start_all(d3, PLANE)
    wait_all(d3, PLANE)

    results = ((dk_stage, dk_out), (dv_stage, dv_out))

    def outgoing(n, j):
        stage, out = results[n]
        to = lax.rem(part + j, PARTS)
        return remote(
            stage.at[to], out.at[:, cols(part)], dkv_send.at[n, j], dkv_recv.at[n, j], mate(to)
        )

    def own_out(n):
        stage, out = results[n]
        return pltpu.make_async_copy(stage.at[part], out.at[:, cols(part)], dkv_recv.at[n, 0])

    for j in (2, 1, 3, 0):
        there = lax.rem(part + j, PARTS)
        for b in range(2):
            span = slice(b * BLOCK, (b + 1) * BLOCK)
            number = there * (2 * GROUPS) + 2 * group + b
            total = acc_own[there, span, :]
            for m in range(GLOBAL):
                extra = h3[m * 4 : (m + 1) * 4].reshape(BLOCK, two).astype(F32)
                named = jnp.full((1, two), gid_ref[m], jnp.int32) == number
                total = total + jnp.where(named, extra, jnp.zeros_like(extra))
            dk_stage[there, span, :] = total[:, 0:W].astype(BF)
            dv_stage[there, span, :] = total[:, W:two].astype(BF)
        for n in range(2):
            if j == 0:
                own_out(n).start()
            else:
                outgoing(n, j).start()

    for copy, count in finish:
        for o in range(1, count):
            copy(o).wait_send()
    for n in range(4):
        for j in range(1, PARTS):
            incoming(n, j).wait_send()
    own_dq().wait()
    for j in range(1, PARTS):
        outgoing_dq(j).wait()
    for n in range(2):
        own_out(n).wait()
        for j in range(1, PARTS):
            outgoing(n, j).wait()


def on_device(queries, key_vectors, value_vectors, output_grad, rand_pick, global_ids):
    rows, width = queries.shape
    out = jax.ShapeDtypeStruct((rows, width), BF)
    anywhere = pl.BlockSpec(memory_space=pl.ANY)
    small = pl.BlockSpec(memory_space=pltpu.SMEM)
    two = 2 * W
    scratch = [
        pltpu.VMEM((PARTS, 2 * BLOCK, W), BF),
        pltpu.VMEM((PARTS, 2 * BLOCK, W), BF),
        pltpu.VMEM((PARTS, 2 * BLOCK, two), BF),
        pltpu.VMEM((PARTS, BLOCK, two), BF),
        pltpu.VMEM((PARTS, BLOCK, two), BF),
        pltpu.VMEM((2, 2 * BLOCK, FULL), BF),
        pltpu.VMEM((PLANE, 16, 2 * FULL), BF),
        pltpu.VMEM((PLANE, 16, 2 * FULL), BF),
        pltpu.VMEM((PARTS, 16, two), BF),
        pltpu.VMEM((PARTS, 16, two), BF),
        pltpu.VMEM((LAYERS, 16, two), BF),
        pltpu.VMEM((GLOBAL * BLOCK, two), BF),
        pltpu.VMEM((PARTS, 2 * BLOCK, two), F32),
        pltpu.VMEM((PARTS, BLOCK, two), F32),
        pltpu.VMEM((PARTS, BLOCK, two), F32),
        pltpu.VMEM((GLOBAL * BLOCK, two), F32),
        pltpu.VMEM((2, PARTS, BLOCK, two), BF),
        pltpu.VMEM((2, PARTS, BLOCK, two), BF),
        pltpu.VMEM((PLANE, 16, two), BF),
        pltpu.VMEM((PLANE, 16, two), BF),
        pltpu.VMEM((LAYERS, 16, two), BF),
        pltpu.VMEM((PLANE, 16, two), BF),
        pltpu.VMEM((PARTS, 2 * BLOCK, W), BF),
        pltpu.VMEM((PARTS, 2 * BLOCK, W), BF),
        pltpu.VMEM((PARTS, 2 * BLOCK, W), BF),
        pltpu.SemaphoreType.DMA((2,)),
        pltpu.SemaphoreType.DMA((4, PARTS)),
        pltpu.SemaphoreType.DMA((4, PARTS)),
        pltpu.SemaphoreType.DMA((4,)),
        pltpu.SemaphoreType.DMA((4,)),
        pltpu.SemaphoreType.DMA((8, PLANE)),
        pltpu.SemaphoreType.DMA((8, PLANE)),
        pltpu.SemaphoreType.DMA((PARTS,)),
        pltpu.SemaphoreType.DMA((PARTS,)),
        pltpu.SemaphoreType.DMA((2, PARTS)),
        pltpu.SemaphoreType.DMA((2, PARTS)),
    ]
    return pl.pallas_call(
        kernel,
        out_shape=(out, out, out),
        in_specs=[anywhere] * 4 + [small] * 2,
        out_specs=(anywhere,) * 3,
        scratch_shapes=scratch,
        compiler_params=pltpu.CompilerParams(
            collective_id=1, has_side_effects=True, vmem_limit_bytes=60 * 1024 * 1024
        ),
        name="sparse_attention_grads",
    )(queries, key_vectors, value_vectors, output_grad, rand_pick.T, global_ids)


def solution(mesh):
    spec = P(("doc", "seq"), None)
    return jax.shard_map(
        on_device,
        mesh=mesh,
        in_specs=(spec, spec, spec, spec, P("doc", None), P("doc")),
        out_specs=(spec, spec, spec),
        check_vma=False,
    )
```

```python
import functools

import jax
import jax.numpy as jnp
from jax import lax
from jax.experimental import pallas as pl
from jax.experimental.pallas import tpu as pltpu
from jax.sharding import PartitionSpec as P

MESH = pl.DeviceIdType.MESH
BLOCK = 64
RAND = 3
GLOBAL = 2
PARTS = 4
PLANE = 8
LAYERS = 4
GROUPS = PLANE * LAYERS
SEQ = PARTS * GROUPS
W = 128
HALF = 64
FULL = PARTS * W
BF = jnp.bfloat16
F32 = jnp.float32


def kernel(
    q_hbm, k_hbm, v_hbm, do_hbm, pick_hbm, gid_hbm,
    dq_out, dk_out, dv_out,
    q_all, do_all, kv_own, kv_left, kv_right,
    kv_raw, cand, g1, g2_out, g2, g3, kv_glob,
    acc_own, acc_left, acc_right, acc_glob,
    edge_out, edge_in, h1_out, h1, h2, h3,
    dq_stage, dk_stage, dv_stage,
    keys_near, q2_all, do2_all, expo_near, gp_near, stats, probs_all, grads_all,
    pick_ref, gid_ref, raw_sem, in_send, in_recv, edge_send, edge_recv, g_send, g_recv,
    dq_send, dq_recv, dkv_send, dkv_recv,
):
    me = lax.axis_index("seq")
    part = lax.div(me, GROUPS)
    group = lax.rem(me, GROUPS)
    layer = lax.div(group, PLANE)
    spot = lax.rem(group, PLANE)

    def mate(quarter):
        return {"seq": quarter * GROUPS + group}

    def in_plane(other):
        return {"seq": part * GROUPS + layer * PLANE + other}

    def in_layer(other):
        return {"seq": part * GROUPS + other * PLANE + spot}

    right = {"seq": part * GROUPS + lax.rem(group + 1, GROUPS)}
    left = {"seq": part * GROUPS + lax.rem(group + GROUPS - 1, GROUPS)}

    barrier = pltpu.get_barrier_semaphore()

    def greet(where):
        pl.semaphore_signal(barrier, inc=1, device_id=where, device_id_type=MESH)

    for j in range(1, PARTS):
        greet(mate(lax.rem(part + j, PARTS)))
    greet(left)
    greet(right)
    for o in range(1, PLANE):
        greet(in_plane(lax.rem(spot + o, PLANE)))
    for o in range(1, LAYERS):
        greet(in_layer(lax.rem(layer + o, LAYERS)))
    def remote(src, dst, send, recv, where):
        return pltpu.make_async_remote_copy(
            src_ref=src, dst_ref=dst, send_sem=send, recv_sem=recv, device_id=where,
            device_id_type=MESH,
        )

    two = 2 * W

    def cols(quarter):
        return pl.ds(pl.multiple_of(quarter * W, W), W)

    arrays = (
        (k_hbm, lambda s: kv_own.at[s, :, 0:W]),
        (v_hbm, lambda s: kv_own.at[s, :, W : 2 * W]),
        (q_hbm, lambda s: q_all.at[s]),
        (do_hbm, lambda s: do_all.at[s]),
    )

    def incoming(n, j):
        hbm, place = arrays[n]
        to = lax.rem(part + j, PARTS)
        return remote(
            hbm.at[:, cols(to)], place(part), in_send.at[n, j], in_recv.at[n, j], mate(to)
        )

    def own_copy(n):
        hbm, place = arrays[n]
        return pltpu.make_async_copy(hbm.at[:, cols(part)], place(part), in_recv.at[n, 0])

    def raw_copy(n):
        return pltpu.make_async_copy((k_hbm, v_hbm)[n], kv_raw.at[n], raw_sem.at[n])

    pick_copy = pltpu.make_async_copy(pick_hbm, pick_ref, raw_sem.at[2])
    gid_copy = pltpu.make_async_copy(gid_hbm, gid_ref, raw_sem.at[3])
    gid_copy.start()
    for n in range(2):
        raw_copy(n).start()
    pick_copy.start()
    for n in range(4):
        own_copy(n).start()

    def choose(code, options):
        code = jnp.full((1, options[0].shape[-1]), code, jnp.int32)
        total = None
        for n, option in enumerate(options):
            option = option.astype(F32)
            term = jnp.where(code == n, option, jnp.zeros_like(option))
            total = term if total is None else total + term
        return total.astype(BF)

    def rows(t):
        return pl.ds(pl.multiple_of(t * 16, 16), 16)

    def around(base, count, here, where, source, place):
        def copy(o):
            to = lax.rem(here + o, count)
            return remote(
                source(to), place(here), g_send.at[base, o], g_recv.at[base, o], where(to)
            )
        return copy

    finish = []

    def start_all(copy, count):
        for o in range(1, count):
            copy(o).start()

    def wait_all(copy, count):
        for o in range(1, count):
            copy(o).wait_recv()
        finish.append((copy, count))

    c1 = around(0, PLANE, spot, in_plane, lambda to: cand.at[to], lambda i: g1.at[i])
    c2 = around(1, PARTS, part, mate, lambda to: g2_out.at[to], lambda i: g2.at[i])
    c3 = around(2, LAYERS, layer, in_layer, lambda to: g3.at[layer], lambda i: g3.at[i])
    c4 = around(
        3, PLANE, spot, in_plane, lambda to: kv_glob.at[rows(spot)], lambda i: kv_glob.at[rows(i)]
    )

    to_right = remote(
        kv_own.at[:, BLOCK : 2 * BLOCK, :], kv_left, edge_send.at[0], edge_recv.at[0], right
    )
    to_left = remote(
        kv_own.at[:, 0:BLOCK, :], kv_right, edge_send.at[1], edge_recv.at[1], left
    )

    pl.semaphore_wait(barrier, PARTS - 1 + 2 + PLANE - 1 + LAYERS - 1)


    def send(n, j):
        incoming(n, j).start()

    send(0, 2)
    gid_copy.wait()
    pick_copy.wait()
    my_gid = gid_ref[lax.div(spot, PLANE // GLOBAL)]
    gid_spot = lax.rem(lax.div(my_gid, 2), PLANE)
    gid_layer = lax.rem(lax.div(my_gid, 2 * PLANE), LAYERS)
    gid_part = lax.div(my_gid, 2 * GROUPS)
    for n in range(2):
        raw_copy(n).wait()
    for t in range(PLANE):
        odd = lax.rem(gid_ref[t // (PLANE // GLOBAL)], 2)
        start = (t % (PLANE // GLOBAL)) * 16
        for n in range(2):
            cand[t, :, n * FULL : (n + 1) * FULL] = choose(
                odd, [kv_raw[n, b * BLOCK + start : b * BLOCK + start + 16, :] for b in range(2)]
            )

    start_all(c1, PLANE)
    send(0, 1)
    send(0, 3)
    g1[spot] = cand[spot]
    wait_all(c1, PLANE)
    piece = choose(gid_spot, [g1[t] for t in range(PLANE)])
    for h in range(PARTS):
        g2_out[h, :, 0:W] = piece[:, h * W : (h + 1) * W]
        g2_out[h, :, W:two] = piece[:, FULL + h * W : FULL + (h + 1) * W]
    start_all(c2, PARTS)
    send(1, 2)
    send(1, 1)
    send(1, 3)
    send(2, 2)
    send(3, 2)
    send(2, 1)
    send(3, 1)
    g2[part] = g2_out[part]
    acc_own[...] = jnp.zeros_like(acc_own)
    acc_left[...] = jnp.zeros_like(acc_left)
    acc_right[...] = jnp.zeros_like(acc_right)
    acc_glob[...] = jnp.zeros_like(acc_glob)
    wait_all(c2, PARTS)
    g3[layer] = choose(gid_part, [g2[t] for t in range(PARTS)])
    start_all(c3, LAYERS)
    send(2, 3)
    send(3, 3)

    for n in range(2):
        own_copy(n).wait()
        for j in (1, 3, 2):
            incoming(n, j).wait_recv()
    to_right.start()
    to_left.start()
    wait_all(c3, LAYERS)
    kv_glob[rows(spot), :] = choose(gid_layer, [g3[t] for t in range(LAYERS)])
    start_all(c4, PLANE)
    first_group = (group == 0).astype(jnp.int32)
    last_group = (group == GROUPS - 1).astype(jnp.int32)
    low = lax.broadcasted_iota(jnp.int32, (BLOCK, W), 1) < HALF

    def two_heads(x):
        x = x.astype(F32)
        zero = jnp.zeros_like(x)
        return jnp.concatenate([jnp.where(low, x, zero), jnp.where(low, zero, x)], axis=0)

    def dot(a, b, dims):
        return lax.dot_general(a, b, (dims, ((), ())), preferred_element_type=F32)

    near = (3 + RAND) * BLOCK

    def quarter_of(t):
        j = t + (t == 1).astype(jnp.int32) - (t == 2).astype(jnp.int32)
        return j, lax.rem(part + PARTS - j, PARTS)

    def entries(here, b):
        at_left = lax.rem(here + (PARTS - 1) * first_group, PARTS)
        at_right = lax.rem(here + last_group, PARTS)
        number = here * (2 * GROUPS) + 2 * group + b
        own0 = (kv_own, here, 0, acc_own)
        own1 = (kv_own, here, BLOCK, acc_own)
        window = [
            (kv_left, at_left, 0, acc_left) if b == 0 else own0,
            own0 if b == 0 else own1,
            own1 if b == 0 else (kv_right, at_right, 0, acc_right),
        ]
        choices = []
        for s in range(RAND):
            far = lax.rem(here + PARTS - (s + 1), PARTS)
            far_left = lax.rem(far + (PARTS - 1) * first_group, PARTS)
            pick = jnp.full((1, two), pick_ref[s, number].astype(F32)).astype(BF)
            near_entry = (kv_own, far, b * BLOCK, acc_own)
            far_entry = (kv_left, far_left, 0, acc_left) if b == 0 else (kv_own, far, 0, acc_own)
            choices.append((near_entry, far_entry, pick))
        return number, window, choices

    def load(entry):
        ref, at, start, _ = entry
        return ref[at, start : start + BLOCK, :]

    def add(entry, value):
        _, at, start, acc = entry
        acc[at, start : start + BLOCK, :] += value

    def own_part(t, _):
        j, here = quarter_of(t)
        for n in (2, 3):
            @pl.when(j == 0)
            def _():
                own_copy(n).wait()

            @pl.when(j != 0)
            def _():
                incoming(n, j).wait_recv()

        for b in range(2):
            at = 2 * t + b
            number, window, choices = entries(here, b)
            pieces = [load(e) for e in window]
            for near_entry, far_entry, pick in choices:
                pieces.append(load(near_entry) * (1 - pick) + load(far_entry) * pick)
            listed = jnp.concatenate(pieces, axis=0)
            keys = listed[:, 0:W]
            values = listed[:, W:two]
            q2 = (two_heads(q_all[here, b * BLOCK : (b + 1) * BLOCK, :]) * 0.125).astype(BF)
            do2 = two_heads(do_all[here, b * BLOCK : (b + 1) * BLOCK, :]).astype(BF)
            scores = dot(keys, q2, ((1,), (1,)))
            edge = 0 if b == 0 else 2
            outside = number == (0 if b == 0 else 2 * SEQ - 1)
            masked = jnp.where(outside, -1e30, scores[edge * BLOCK : (edge + 1) * BLOCK])
            ahead = [scores[: edge * BLOCK]] if b else []
            scores = jnp.concatenate(ahead + [masked, scores[(edge + 1) * BLOCK :]], axis=0)
            row_max = jnp.max(scores, axis=0, keepdims=True)
            expo = jnp.exp(scores - row_max)
            keys_near[at] = keys
            q2_all[at] = q2
            do2_all[at] = do2
            expo_near[at] = expo
            gp_near[at] = dot(values, do2, ((1,), (1,)))
            stats[at, 0:1, :] = row_max
            stats[at, 1:2, :] = jnp.sum(expo, axis=0, keepdims=True)
        return 0

    def whole_rows(t, _):
        keys = kv_glob[:, 0:W]
        values = kv_glob[:, W:two]
        for b in range(2):
            at = 2 * t + b
            q2 = q2_all[at]
            do2 = do2_all[at]
            scores = dot(keys, q2, ((1,), (1,)))
            grad_probs = dot(values, do2, ((1,), (1,)))
            near_max = stats[at, 0:1, :]
            row_max = jnp.maximum(near_max, jnp.max(scores, axis=0, keepdims=True))
            shrink = jnp.exp(near_max - row_max)
            expo = jnp.exp(scores - row_max)
            row_total = stats[at, 1:2, :] * shrink + jnp.sum(expo, axis=0, keepdims=True)
            inverse = 1.0 / row_total
            probs = expo * inverse
            probs_half = probs.astype(BF)
            probs_near = expo_near[at] * (shrink * inverse)
            half_near = probs_near.astype(BF)
            gp = gp_near[at]
            row_dot = jnp.sum(probs_half.astype(F32) * grad_probs, axis=0, keepdims=True) + jnp.sum(
                half_near.astype(F32) * gp, axis=0, keepdims=True
            )
            grad_half = (probs * (grad_probs - row_dot)).astype(BF)
            probs_all[at] = half_near
            grads_all[at, 0:near, :] = (probs_near * (gp - row_dot)).astype(BF)
            grads_all[at, near:, :] = grad_half
            acc_glob[:, 0:W] += dot(grad_half, q2, ((1,), (0,)))
            acc_glob[:, W:two] += dot(probs_half, do2, ((1,), (0,)))
        return 0

    def spread(t, _):
        _, here = quarter_of(t)
        for b in range(2):
            at = 2 * t + b
            _, window, choices = entries(here, b)
            grad_near = grads_all[at, 0:near, :]
            back = dot(grad_near, keys_near[at], ((0,), (0,))) + dot(
                grads_all[at, near:, :], kv_glob[:, 0:W], ((0,), (0,))
            )
            dq_stage[here, b * BLOCK : (b + 1) * BLOCK, :] = (
                jnp.where(low, back[:BLOCK], back[BLOCK:]) * 0.125
            ).astype(BF)
            grads = jnp.concatenate(
                [
                    dot(grad_near, q2_all[at], ((1,), (0,))),
                    dot(probs_all[at], do2_all[at], ((1,), (0,))),
                ],
                axis=1,
            )
            for n, entry in enumerate(window):
                add(entry, grads[n * BLOCK : (n + 1) * BLOCK])
            for n, (near_entry, far_entry, pick) in enumerate(choices):
                part_grad = grads[(3 + n) * BLOCK : (4 + n) * BLOCK]
                far_grad = part_grad * pick.astype(F32)
                add(near_entry, part_grad - far_grad)
                add(far_entry, far_grad)
        return 0

    def outgoing_dq(j):
        to = lax.rem(part + j, PARTS)
        return remote(
            dq_stage.at[to], dq_out.at[:, cols(part)], dq_send.at[j], dq_recv.at[j], mate(to)
        )

    def own_dq():
        return pltpu.make_async_copy(dq_stage.at[part], dq_out.at[:, cols(part)], dq_recv.at[0])

    to_right.wait()
    to_left.wait()
    lax.fori_loop(0, PARTS, own_part, 0)
    wait_all(c4, PLANE)
    lax.fori_loop(0, PARTS, whole_rows, 0)

    d1 = around(4, PLANE, spot, in_plane, lambda to: h1_out.at[to], lambda i: h1.at[i])
    d2 = around(5, LAYERS, layer, in_layer, lambda to: h2.at[layer], lambda i: h2.at[i])
    d3 = around(6, PLANE, spot, in_plane, lambda to: h3.at[spot], lambda i: h3.at[i])

    for t in range(PLANE):
        h1_out[t] = acc_glob[t * 16 : (t + 1) * 16, :].astype(BF)
    start_all(d1, PLANE)
    h1[spot] = h1_out[spot]
    lax.fori_loop(0, PARTS, spread, 0)
    own_dq().start()
    wait_all(d1, PLANE)
    h2[layer] = jnp.sum(h1[...].astype(F32), axis=0).astype(BF)
    start_all(d2, LAYERS)
    edge_out[0] = acc_left[...].astype(BF)
    edge_out[1] = acc_right[...].astype(BF)
    back_left = remote(edge_out.at[0], edge_in.at[0], edge_send.at[2], edge_recv.at[2], left)
    back_right = remote(edge_out.at[1], edge_in.at[1], edge_send.at[3], edge_recv.at[3], right)
    back_left.start()
    back_right.start()
    wait_all(d2, LAYERS)
    h3[spot] = jnp.sum(h2[...].astype(F32), axis=0).astype(BF)
    start_all(d3, PLANE)
    outgoing_dq(2).start()
    outgoing_dq(1).start()
    outgoing_dq(3).start()
    back_left.wait()
    back_right.wait()
    for b in range(2):
        acc_own[:, b * BLOCK : (b + 1) * BLOCK, :] += edge_in[1 - b].astype(F32)
    wait_all(d3, PLANE)

    results = ((dk_stage, dk_out), (dv_stage, dv_out))

    def outgoing(n, j):
        stage, out = results[n]
        to = lax.rem(part + j, PARTS)
        return remote(
            stage.at[to], out.at[:, cols(part)], dkv_send.at[n, j], dkv_recv.at[n, j], mate(to)
        )

    def own_out(n):
        stage, out = results[n]
        return pltpu.make_async_copy(stage.at[part], out.at[:, cols(part)], dkv_recv.at[n, 0])

    for j in (2, 1, 3, 0):
        there = lax.rem(part + j, PARTS)
        for b in range(2):
            span = slice(b * BLOCK, (b + 1) * BLOCK)
            number = there * (2 * GROUPS) + 2 * group + b
            total = acc_own[there, span, :]
            for m in range(GLOBAL):
                extra = h3[m * 4 : (m + 1) * 4].reshape(BLOCK, two).astype(F32)
                named = jnp.full((1, two), gid_ref[m], jnp.int32) == number
                total = total + jnp.where(named, extra, jnp.zeros_like(extra))
            dk_stage[there, span, :] = total[:, 0:W].astype(BF)
            dv_stage[there, span, :] = total[:, W:two].astype(BF)
        for n in range(2):
            if j == 0:
                own_out(n).start()
            else:
                outgoing(n, j).start()

    for copy, count in finish:
        for o in range(1, count):
            copy(o).wait_send()
    for n in range(4):
        for j in range(1, PARTS):
            incoming(n, j).wait_send()
    own_dq().wait()
    for j in range(1, PARTS):
        outgoing_dq(j).wait()
    for n in range(2):
        own_out(n).wait()
        for j in range(1, PARTS):
            outgoing(n, j).wait()


def on_device(queries, key_vectors, value_vectors, output_grad, rand_pick, global_ids):
    rows, width = queries.shape
    out = jax.ShapeDtypeStruct((rows, width), BF)
    anywhere = pl.BlockSpec(memory_space=pl.ANY)
    two = 2 * W
    scratch = [
        pltpu.VMEM((PARTS, 2 * BLOCK, W), BF),
        pltpu.VMEM((PARTS, 2 * BLOCK, W), BF),
        pltpu.VMEM((PARTS, 2 * BLOCK, two), BF),
        pltpu.VMEM((PARTS, BLOCK, two), BF),
        pltpu.VMEM((PARTS, BLOCK, two), BF),
        pltpu.VMEM((2, 2 * BLOCK, FULL), BF),
        pltpu.VMEM((PLANE, 16, 2 * FULL), BF),
        pltpu.VMEM((PLANE, 16, 2 * FULL), BF),
        pltpu.VMEM((PARTS, 16, two), BF),
        pltpu.VMEM((PARTS, 16, two), BF),
        pltpu.VMEM((LAYERS, 16, two), BF),
        pltpu.VMEM((GLOBAL * BLOCK, two), BF),
        pltpu.VMEM((PARTS, 2 * BLOCK, two), F32),
        pltpu.VMEM((PARTS, BLOCK, two), F32),
        pltpu.VMEM((PARTS, BLOCK, two), F32),
        pltpu.VMEM((GLOBAL * BLOCK, two), F32),
        pltpu.VMEM((2, PARTS, BLOCK, two), BF),
        pltpu.VMEM((2, PARTS, BLOCK, two), BF),
        pltpu.VMEM((PLANE, 16, two), BF),
        pltpu.VMEM((PLANE, 16, two), BF),
        pltpu.VMEM((LAYERS, 16, two), BF),
        pltpu.VMEM((PLANE, 16, two), BF),
        pltpu.VMEM((PARTS, 2 * BLOCK, W), BF),
        pltpu.VMEM((PARTS, 2 * BLOCK, W), BF),
        pltpu.VMEM((PARTS, 2 * BLOCK, W), BF),
        pltpu.VMEM((2 * PARTS, 6 * BLOCK, W), BF),
        pltpu.VMEM((2 * PARTS, 2 * BLOCK, W), BF),
        pltpu.VMEM((2 * PARTS, 2 * BLOCK, W), BF),
        pltpu.VMEM((2 * PARTS, 6 * BLOCK, W), F32),
        pltpu.VMEM((2 * PARTS, 6 * BLOCK, W), F32),
        pltpu.VMEM((2 * PARTS, 8, W), F32),
        pltpu.VMEM((2 * PARTS, 6 * BLOCK, W), BF),
        pltpu.VMEM((2 * PARTS, 8 * BLOCK, W), BF),
        pltpu.SMEM((RAND, 2 * SEQ), jnp.int32),
        pltpu.SMEM((GLOBAL,), jnp.int32),
        pltpu.SemaphoreType.DMA((4,)),
        pltpu.SemaphoreType.DMA((4, PARTS)),
        pltpu.SemaphoreType.DMA((4, PARTS)),
        pltpu.SemaphoreType.DMA((4,)),
        pltpu.SemaphoreType.DMA((4,)),
        pltpu.SemaphoreType.DMA((8, PLANE)),
        pltpu.SemaphoreType.DMA((8, PLANE)),
        pltpu.SemaphoreType.DMA((PARTS,)),
        pltpu.SemaphoreType.DMA((PARTS,)),
        pltpu.SemaphoreType.DMA((2, PARTS)),
        pltpu.SemaphoreType.DMA((2, PARTS)),
    ]
    return pl.pallas_call(
        kernel,
        out_shape=(out, out, out),
        in_specs=[anywhere] * 6,
        out_specs=(anywhere,) * 3,
        scratch_shapes=scratch,
        compiler_params=pltpu.CompilerParams(
            collective_id=1, has_side_effects=True, vmem_limit_bytes=60 * 1024 * 1024
        ),
        name="sparse_attention_grads",
    )(queries, key_vectors, value_vectors, output_grad, rand_pick.T, global_ids)


def solution(mesh):
    spec = P(("doc", "seq"), None)
    return jax.shard_map(
        on_device,
        mesh=mesh,
        in_specs=(spec, spec, spec, spec, P("doc", None), P("doc")),
        out_specs=(spec, spec, spec),
        check_vma=False,
    )
```

```python
import functools

import jax
import jax.numpy as jnp
from jax import lax
from jax.experimental import pallas as pl
from jax.experimental.pallas import tpu as pltpu
from jax.sharding import PartitionSpec as P

MESH = pl.DeviceIdType.MESH
BLOCK = 64
RAND = 3
GLOBAL = 2
PARTS = 4
PLANE = 8
LAYERS = 4
GROUPS = PLANE * LAYERS
SEQ = PARTS * GROUPS
W = 128
HALF = 64
FULL = PARTS * W
BF = jnp.bfloat16
F32 = jnp.float32


def kernel(
    q_hbm, k_hbm, v_hbm, do_hbm, pick_hbm, gid_hbm,
    grads_out,
    q_all, do_all, kv_own, kv_left, kv_right,
    kv_raw, cand, g1, g2_out, g2, g3, kv_glob,
    acc_own, acc_left, acc_right, acc_glob,
    edge_out, edge_in, h1_out, h1, h2, h3,
    dq_stage, dk_stage, dv_stage,
    keys_near, q2_all, do2_all, expo_near, gp_near, stats, probs_all, grads_all,
    pick_ref, gid_ref, raw_sem, in_send, in_recv, edge_send, edge_recv, g_send, g_recv,
    dq_send, dq_recv, dkv_send, dkv_recv,
):
    me = lax.axis_index("seq")
    dq_out, dk_out, dv_out = (grads_out.at[n] for n in range(3))
    part = lax.div(me, GROUPS)
    group = lax.rem(me, GROUPS)
    layer = lax.div(group, PLANE)
    spot = lax.rem(group, PLANE)

    def mate(quarter):
        return {"seq": quarter * GROUPS + group}

    def in_plane(other):
        return {"seq": part * GROUPS + layer * PLANE + other}

    def in_layer(other):
        return {"seq": part * GROUPS + other * PLANE + spot}

    right = {"seq": part * GROUPS + lax.rem(group + 1, GROUPS)}
    left = {"seq": part * GROUPS + lax.rem(group + GROUPS - 1, GROUPS)}

    barrier = pltpu.get_barrier_semaphore()

    def greet(where):
        pl.semaphore_signal(barrier, inc=1, device_id=where, device_id_type=MESH)

    for j in range(1, PARTS):
        greet(mate(lax.rem(part + j, PARTS)))
    greet(left)
    greet(right)
    for o in range(1, PLANE):
        greet(in_plane(lax.rem(spot + o, PLANE)))
    for o in range(1, LAYERS):
        greet(in_layer(lax.rem(layer + o, LAYERS)))
    def remote(src, dst, send, recv, where):
        return pltpu.make_async_remote_copy(
            src_ref=src, dst_ref=dst, send_sem=send, recv_sem=recv, device_id=where,
            device_id_type=MESH,
        )

    two = 2 * W

    def cols(quarter):
        return pl.ds(pl.multiple_of(quarter * W, W), W)

    arrays = (
        (k_hbm, lambda s: kv_own.at[s, :, 0:W]),
        (v_hbm, lambda s: kv_own.at[s, :, W : 2 * W]),
        (q_hbm, lambda s: q_all.at[s]),
        (do_hbm, lambda s: do_all.at[s]),
    )

    def incoming(n, j):
        hbm, place = arrays[n]
        to = lax.rem(part + j, PARTS)
        return remote(
            hbm.at[:, cols(to)], place(part), in_send.at[n, j], in_recv.at[n, j], mate(to)
        )

    def own_copy(n):
        hbm, place = arrays[n]
        return pltpu.make_async_copy(hbm.at[:, cols(part)], place(part), in_recv.at[n, 0])

    def raw_copy(n):
        return pltpu.make_async_copy((k_hbm, v_hbm)[n], kv_raw.at[n], raw_sem.at[n])

    pick_copy = pltpu.make_async_copy(pick_hbm, pick_ref, raw_sem.at[2])
    gid_copy = pltpu.make_async_copy(gid_hbm, gid_ref, raw_sem.at[3])
    gid_copy.start()
    for n in range(2):
        raw_copy(n).start()
    pick_copy.start()
    for n in range(4):
        own_copy(n).start()

    def choose(code, options):
        code = jnp.full((1, options[0].shape[-1]), code, jnp.int32)
        total = None
        for n, option in enumerate(options):
            option = option.astype(F32)
            term = jnp.where(code == n, option, jnp.zeros_like(option))
            total = term if total is None else total + term
        return total.astype(BF)

    def rows(t):
        return pl.ds(pl.multiple_of(t * 16, 16), 16)

    def around(base, count, here, where, source, place):
        def copy(o):
            to = lax.rem(here + o, count)
            return remote(
                source(to), place(here), g_send.at[base, o], g_recv.at[base, o], where(to)
            )
        return copy

    finish = []

    def start_all(copy, count):
        for o in range(1, count):
            copy(o).start()

    def wait_all(copy, count):
        for o in range(1, count):
            copy(o).wait_recv()
        finish.append((copy, count))

    c1 = around(0, PLANE, spot, in_plane, lambda to: cand.at[to], lambda i: g1.at[i])
    c2 = around(1, PARTS, part, mate, lambda to: g2_out.at[to], lambda i: g2.at[i])
    c3 = around(2, LAYERS, layer, in_layer, lambda to: g3.at[layer], lambda i: g3.at[i])
    c4 = around(
        3, PLANE, spot, in_plane, lambda to: kv_glob.at[rows(spot)], lambda i: kv_glob.at[rows(i)]
    )

    to_right = remote(
        kv_own.at[:, BLOCK : 2 * BLOCK, :], kv_left, edge_send.at[0], edge_recv.at[0], right
    )
    to_left = remote(
        kv_own.at[:, 0:BLOCK, :], kv_right, edge_send.at[1], edge_recv.at[1], left
    )

    pl.semaphore_wait(barrier, PARTS - 1 + 2 + PLANE - 1 + LAYERS - 1)


    def send(n, j):
        incoming(n, j).start()

    send(0, 2)
    gid_copy.wait()
    pick_copy.wait()
    my_gid = gid_ref[lax.div(spot, PLANE // GLOBAL)]
    gid_spot = lax.rem(lax.div(my_gid, 2), PLANE)
    gid_layer = lax.rem(lax.div(my_gid, 2 * PLANE), LAYERS)
    gid_part = lax.div(my_gid, 2 * GROUPS)
    for n in range(2):
        raw_copy(n).wait()
    for t in range(PLANE):
        odd = lax.rem(gid_ref[t // (PLANE // GLOBAL)], 2)
        start = (t % (PLANE // GLOBAL)) * 16
        for n in range(2):
            cand[t, :, n * FULL : (n + 1) * FULL] = choose(
                odd, [kv_raw[n, b * BLOCK + start : b * BLOCK + start + 16, :] for b in range(2)]
            )

    start_all(c1, PLANE)
    send(0, 1)
    send(0, 3)
    g1[spot] = cand[spot]
    wait_all(c1, PLANE)
    piece = choose(gid_spot, [g1[t] for t in range(PLANE)])
    for h in range(PARTS):
        g2_out[h, :, 0:W] = piece[:, h * W : (h + 1) * W]
        g2_out[h, :, W:two] = piece[:, FULL + h * W : FULL + (h + 1) * W]
    start_all(c2, PARTS)
    send(1, 2)
    send(1, 1)
    send(1, 3)
    send(2, 2)
    send(3, 2)
    send(2, 1)
    send(3, 1)
    send(2, 3)
    g2[part] = g2_out[part]
    acc_own[...] = jnp.zeros_like(acc_own)
    acc_left[...] = jnp.zeros_like(acc_left)
    acc_right[...] = jnp.zeros_like(acc_right)
    acc_glob[...] = jnp.zeros_like(acc_glob)
    wait_all(c2, PARTS)
    g3[layer] = choose(gid_part, [g2[t] for t in range(PARTS)])
    start_all(c3, LAYERS)
    send(3, 3)

    for n in range(2):
        own_copy(n).wait()
        for j in (1, 3, 2):
            incoming(n, j).wait_recv()
    to_right.start()
    to_left.start()
    wait_all(c3, LAYERS)
    kv_glob[rows(spot), :] = choose(gid_layer, [g3[t] for t in range(LAYERS)])
    start_all(c4, PLANE)
    first_group = (group == 0).astype(jnp.int32)
    last_group = (group == GROUPS - 1).astype(jnp.int32)
    low = lax.broadcasted_iota(jnp.int32, (BLOCK, W), 1) < HALF

    def two_heads(x):
        x = x.astype(F32)
        zero = jnp.zeros_like(x)
        return jnp.concatenate([jnp.where(low, x, zero), jnp.where(low, zero, x)], axis=0)

    def dot(a, b, dims):
        return lax.dot_general(a, b, (dims, ((), ())), preferred_element_type=F32)

    near = (3 + RAND) * BLOCK

    def quarter_of(t):
        j = t + (t == 1).astype(jnp.int32) - (t == 2).astype(jnp.int32)
        return j, lax.rem(part + PARTS - j, PARTS)

    def entries(here, b):
        at_left = lax.rem(here + (PARTS - 1) * first_group, PARTS)
        at_right = lax.rem(here + last_group, PARTS)
        number = here * (2 * GROUPS) + 2 * group + b
        own0 = (kv_own, here, 0, acc_own)
        own1 = (kv_own, here, BLOCK, acc_own)
        window = [
            (kv_left, at_left, 0, acc_left) if b == 0 else own0,
            own0 if b == 0 else own1,
            own1 if b == 0 else (kv_right, at_right, 0, acc_right),
        ]
        choices = []
        for s in range(RAND):
            far = lax.rem(here + PARTS - (s + 1), PARTS)
            far_left = lax.rem(far + (PARTS - 1) * first_group, PARTS)
            pick = jnp.full((1, two), pick_ref[s, number].astype(F32)).astype(BF)
            near_entry = (kv_own, far, b * BLOCK, acc_own)
            far_entry = (kv_left, far_left, 0, acc_left) if b == 0 else (kv_own, far, 0, acc_own)
            choices.append((near_entry, far_entry, pick))
        return number, window, choices

    def load(entry):
        ref, at, start, _ = entry
        return ref[at, start : start + BLOCK, :]

    def add(entry, value):
        _, at, start, acc = entry
        acc[at, start : start + BLOCK, :] += value

    def own_part(t, _):
        j, here = quarter_of(t)
        for n in (2, 3):
            @pl.when(j == 0)
            def _():
                own_copy(n).wait()

            @pl.when(j != 0)
            def _():
                incoming(n, j).wait_recv()

        for b in range(2):
            at = 2 * t + b
            number, window, choices = entries(here, b)
            pieces = [load(e) for e in window]
            for near_entry, far_entry, pick in choices:
                pieces.append(load(near_entry) * (1 - pick) + load(far_entry) * pick)
            listed = jnp.concatenate(pieces, axis=0)
            keys = listed[:, 0:W]
            values = listed[:, W:two]
            q2 = (two_heads(q_all[here, b * BLOCK : (b + 1) * BLOCK, :]) * 0.125).astype(BF)
            do2 = two_heads(do_all[here, b * BLOCK : (b + 1) * BLOCK, :]).astype(BF)
            scores = dot(keys, q2, ((1,), (1,)))
            edge = 0 if b == 0 else 2
            outside = number == (0 if b == 0 else 2 * SEQ - 1)
            masked = jnp.where(outside, -1e30, scores[edge * BLOCK : (edge + 1) * BLOCK])
            ahead = [scores[: edge * BLOCK]] if b else []
            scores = jnp.concatenate(ahead + [masked, scores[(edge + 1) * BLOCK :]], axis=0)
            row_max = jnp.max(scores, axis=0, keepdims=True)
            expo = jnp.exp(scores - row_max)
            keys_near[at] = keys
            q2_all[at] = q2
            do2_all[at] = do2
            expo_near[at] = expo
            gp_near[at] = dot(values, do2, ((1,), (1,)))
            stats[at, 0:1, :] = row_max
            stats[at, 1:2, :] = jnp.sum(expo, axis=0, keepdims=True)
        return 0

    def whole_rows(t, _):
        keys = kv_glob[:, 0:W]
        values = kv_glob[:, W:two]
        for b in range(2):
            at = 2 * t + b
            q2 = q2_all[at]
            do2 = do2_all[at]
            scores = dot(keys, q2, ((1,), (1,)))
            grad_probs = dot(values, do2, ((1,), (1,)))
            near_max = stats[at, 0:1, :]
            row_max = jnp.maximum(near_max, jnp.max(scores, axis=0, keepdims=True))
            shrink = jnp.exp(near_max - row_max)
            expo = jnp.exp(scores - row_max)
            row_total = stats[at, 1:2, :] * shrink + jnp.sum(expo, axis=0, keepdims=True)
            inverse = 1.0 / row_total
            probs = expo * inverse
            probs_half = probs.astype(BF)
            probs_near = expo_near[at] * (shrink * inverse)
            half_near = probs_near.astype(BF)
            gp = gp_near[at]
            row_dot = jnp.sum(probs_half.astype(F32) * grad_probs, axis=0, keepdims=True) + jnp.sum(
                half_near.astype(F32) * gp, axis=0, keepdims=True
            )
            grad_half = (probs * (grad_probs - row_dot)).astype(BF)
            probs_all[at] = half_near
            grads_all[at, 0:near, :] = (probs_near * (gp - row_dot)).astype(BF)
            grads_all[at, near:, :] = grad_half
            acc_glob[:, 0:W] += dot(grad_half, q2, ((1,), (0,)))
            acc_glob[:, W:two] += dot(probs_half, do2, ((1,), (0,)))
        return 0

    def spread(t, _):
        _, here = quarter_of(t)
        for b in range(2):
            at = 2 * t + b
            _, window, choices = entries(here, b)
            grad_near = grads_all[at, 0:near, :]
            back = dot(grad_near, keys_near[at], ((0,), (0,))) + dot(
                grads_all[at, near:, :], kv_glob[:, 0:W], ((0,), (0,))
            )
            dq_stage[here, b * BLOCK : (b + 1) * BLOCK, :] = (
                jnp.where(low, back[:BLOCK], back[BLOCK:]) * 0.125
            ).astype(BF)
            grads = jnp.concatenate(
                [
                    dot(grad_near, q2_all[at], ((1,), (0,))),
                    dot(probs_all[at], do2_all[at], ((1,), (0,))),
                ],
                axis=1,
            )
            for n, entry in enumerate(window):
                add(entry, grads[n * BLOCK : (n + 1) * BLOCK])
            for n, (near_entry, far_entry, pick) in enumerate(choices):
                part_grad = grads[(3 + n) * BLOCK : (4 + n) * BLOCK]
                far_grad = part_grad * pick.astype(F32)
                add(near_entry, part_grad - far_grad)
                add(far_entry, far_grad)
        return 0

    def outgoing_dq(j):
        to = lax.rem(part + j, PARTS)
        return remote(
            dq_stage.at[to], dq_out.at[:, cols(part)], dq_send.at[j], dq_recv.at[j], mate(to)
        )

    def own_dq():
        return pltpu.make_async_copy(dq_stage.at[part], dq_out.at[:, cols(part)], dq_recv.at[0])

    to_right.wait()
    to_left.wait()
    lax.fori_loop(0, PARTS, own_part, 0)
    wait_all(c4, PLANE)
    lax.fori_loop(0, PARTS, whole_rows, 0, unroll=True)

    d1 = around(4, PLANE, spot, in_plane, lambda to: h1_out.at[to], lambda i: h1.at[i])
    d2 = around(5, LAYERS, layer, in_layer, lambda to: h2.at[layer], lambda i: h2.at[i])
    d3 = around(6, PLANE, spot, in_plane, lambda to: h3.at[spot], lambda i: h3.at[i])

    for t in range(PLANE):
        h1_out[t] = acc_glob[t * 16 : (t + 1) * 16, :].astype(BF)
    start_all(d1, PLANE)
    h1[spot] = h1_out[spot]
    lax.fori_loop(0, PARTS, spread, 0)
    own_dq().start()
    wait_all(d1, PLANE)
    h2[layer] = jnp.sum(h1[...].astype(F32), axis=0).astype(BF)
    start_all(d2, LAYERS)
    edge_out[0] = acc_left[...].astype(BF)
    edge_out[1] = acc_right[...].astype(BF)
    back_left = remote(edge_out.at[0], edge_in.at[0], edge_send.at[2], edge_recv.at[2], left)
    back_right = remote(edge_out.at[1], edge_in.at[1], edge_send.at[3], edge_recv.at[3], right)
    back_left.start()
    back_right.start()
    wait_all(d2, LAYERS)
    h3[spot] = jnp.sum(h2[...].astype(F32), axis=0).astype(BF)
    start_all(d3, PLANE)
    outgoing_dq(2).start()
    outgoing_dq(1).start()
    outgoing_dq(3).start()
    back_left.wait()
    back_right.wait()
    for b in range(2):
        acc_own[:, b * BLOCK : (b + 1) * BLOCK, :] += edge_in[1 - b].astype(F32)
    wait_all(d3, PLANE)

    results = ((dk_stage, dk_out), (dv_stage, dv_out))

    def outgoing(n, j):
        stage, out = results[n]
        to = lax.rem(part + j, PARTS)
        return remote(
            stage.at[to], out.at[:, cols(part)], dkv_send.at[n, j], dkv_recv.at[n, j], mate(to)
        )

    def own_out(n):
        stage, out = results[n]
        return pltpu.make_async_copy(stage.at[part], out.at[:, cols(part)], dkv_recv.at[n, 0])

    for j in (2, 1, 3, 0):
        there = lax.rem(part + j, PARTS)
        for b in range(2):
            span = slice(b * BLOCK, (b + 1) * BLOCK)
            number = there * (2 * GROUPS) + 2 * group + b
            total = acc_own[there, span, :]
            for m in range(GLOBAL):
                extra = h3[m * 4 : (m + 1) * 4].reshape(BLOCK, two).astype(F32)
                named = jnp.full((1, two), gid_ref[m], jnp.int32) == number
                total = total + jnp.where(named, extra, jnp.zeros_like(extra))
            dk_stage[there, span, :] = total[:, 0:W].astype(BF)
            dv_stage[there, span, :] = total[:, W:two].astype(BF)
        for n in range(2):
            if j == 0:
                own_out(n).start()
            else:
                outgoing(n, j).start()

    for copy, count in finish:
        for o in range(1, count):
            copy(o).wait_send()
    for n in range(4):
        for j in range(1, PARTS):
            incoming(n, j).wait_send()
    own_dq().wait()
    for j in range(1, PARTS):
        outgoing_dq(j).wait()
    for n in range(2):
        own_out(n).wait()
        for j in range(1, PARTS):
            outgoing(n, j).wait()


def on_device(queries, key_vectors, value_vectors, output_grad, rand_pick, global_ids):
    rows, width = queries.shape
    out = jax.ShapeDtypeStruct((3, rows, width), BF)
    anywhere = pl.BlockSpec(memory_space=pl.ANY)
    two = 2 * W
    scratch = [
        pltpu.VMEM((PARTS, 2 * BLOCK, W), BF),
        pltpu.VMEM((PARTS, 2 * BLOCK, W), BF),
        pltpu.VMEM((PARTS, 2 * BLOCK, two), BF),
        pltpu.VMEM((PARTS, BLOCK, two), BF),
        pltpu.VMEM((PARTS, BLOCK, two), BF),
        pltpu.VMEM((2, 2 * BLOCK, FULL), BF),
        pltpu.VMEM((PLANE, 16, 2 * FULL), BF),
        pltpu.VMEM((PLANE, 16, 2 * FULL), BF),
        pltpu.VMEM((PARTS, 16, two), BF),
        pltpu.VMEM((PARTS, 16, two), BF),
        pltpu.VMEM((LAYERS, 16, two), BF),
        pltpu.VMEM((GLOBAL * BLOCK, two), BF),
        pltpu.VMEM((PARTS, 2 * BLOCK, two), F32),
        pltpu.VMEM((PARTS, BLOCK, two), F32),
        pltpu.VMEM((PARTS, BLOCK, two), F32),
        pltpu.VMEM((GLOBAL * BLOCK, two), F32),
        pltpu.VMEM((2, PARTS, BLOCK, two), BF),
        pltpu.VMEM((2, PARTS, BLOCK, two), BF),
        pltpu.VMEM((PLANE, 16, two), BF),
        pltpu.VMEM((PLANE, 16, two), BF),
        pltpu.VMEM((LAYERS, 16, two), BF),
        pltpu.VMEM((PLANE, 16, two), BF),
        pltpu.VMEM((PARTS, 2 * BLOCK, W), BF),
        pltpu.VMEM((PARTS, 2 * BLOCK, W), BF),
        pltpu.VMEM((PARTS, 2 * BLOCK, W), BF),
        pltpu.VMEM((2 * PARTS, 6 * BLOCK, W), BF),
        pltpu.VMEM((2 * PARTS, 2 * BLOCK, W), BF),
        pltpu.VMEM((2 * PARTS, 2 * BLOCK, W), BF),
        pltpu.VMEM((2 * PARTS, 6 * BLOCK, W), F32),
        pltpu.VMEM((2 * PARTS, 6 * BLOCK, W), F32),
        pltpu.VMEM((2 * PARTS, 8, W), F32),
        pltpu.VMEM((2 * PARTS, 6 * BLOCK, W), BF),
        pltpu.VMEM((2 * PARTS, 8 * BLOCK, W), BF),
        pltpu.SMEM((RAND, 2 * SEQ), jnp.int32),
        pltpu.SMEM((GLOBAL,), jnp.int32),
        pltpu.SemaphoreType.DMA((4,)),
        pltpu.SemaphoreType.DMA((4, PARTS)),
        pltpu.SemaphoreType.DMA((4, PARTS)),
        pltpu.SemaphoreType.DMA((4,)),
        pltpu.SemaphoreType.DMA((4,)),
        pltpu.SemaphoreType.DMA((8, PLANE)),
        pltpu.SemaphoreType.DMA((8, PLANE)),
        pltpu.SemaphoreType.DMA((PARTS,)),
        pltpu.SemaphoreType.DMA((PARTS,)),
        pltpu.SemaphoreType.DMA((2, PARTS)),
        pltpu.SemaphoreType.DMA((2, PARTS)),
    ]
    grads = pl.pallas_call(
        kernel,
        out_shape=out,
        in_specs=[anywhere] * 6,
        out_specs=anywhere,
        scratch_shapes=scratch,
        compiler_params=pltpu.CompilerParams(
            collective_id=1, has_side_effects=True, vmem_limit_bytes=60 * 1024 * 1024
        ),
        name="sparse_attention_grads",
    )(queries, key_vectors, value_vectors, output_grad, rand_pick.T, global_ids)
    return grads[0], grads[1], grads[2]


def solution(mesh):
    spec = P(("doc", "seq"), None)
    return jax.shard_map(
        on_device,
        mesh=mesh,
        in_specs=(spec, spec, spec, spec, P("doc", None), P("doc")),
        out_specs=(spec, spec, spec),
        check_vma=False,
    )
```

```python
import functools

import jax
import jax.numpy as jnp
from jax import lax
from jax.experimental import pallas as pl
from jax.experimental.pallas import tpu as pltpu
from jax.sharding import PartitionSpec as P

MESH = pl.DeviceIdType.MESH
BLOCK = 64
RAND = 3
GLOBAL = 2
PARTS = 4
PLANE = 8
LAYERS = 4
GROUPS = PLANE * LAYERS
SEQ = PARTS * GROUPS
W = 128
HALF = 64
FULL = PARTS * W
BF = jnp.bfloat16
F32 = jnp.float32


def kernel(
    q_hbm, k_hbm, v_hbm, do_hbm, pick_hbm, gid_hbm,
    grads_out,
    q_all, do_all, kv_own, kv_left, kv_right,
    kv_raw, cand, g1, g2_out, g2, g3, kv_glob,
    acc_own, acc_left, acc_right,
    edge_out, edge_in, h1_out, h1, h2, h3,
    dq_stage, dk_stage, dv_stage,
    keys_near, q2_all, do2_all, expo_near, gp_near, stats, probs_all, grads_all,
    probs_glob, grads_glob,
    pick_ref, gid_ref, raw_sem, in_send, in_recv, edge_send, edge_recv, g_send, g_recv,
    dq_send, dq_recv, dkv_send, dkv_recv,
):
    me = lax.axis_index("seq")
    dq_out, dk_out, dv_out = (grads_out.at[n] for n in range(3))
    part = lax.div(me, GROUPS)
    group = lax.rem(me, GROUPS)
    layer = lax.div(group, PLANE)
    spot = lax.rem(group, PLANE)

    def mate(quarter):
        return {"seq": quarter * GROUPS + group}

    def in_plane(other):
        return {"seq": part * GROUPS + layer * PLANE + other}

    def in_layer(other):
        return {"seq": part * GROUPS + other * PLANE + spot}

    right = {"seq": part * GROUPS + lax.rem(group + 1, GROUPS)}
    left = {"seq": part * GROUPS + lax.rem(group + GROUPS - 1, GROUPS)}

    barrier = pltpu.get_barrier_semaphore()

    def greet(where):
        pl.semaphore_signal(barrier, inc=1, device_id=where, device_id_type=MESH)

    for j in range(1, PARTS):
        greet(mate(lax.rem(part + j, PARTS)))
    greet(left)
    greet(right)
    for o in range(1, PLANE):
        greet(in_plane(lax.rem(spot + o, PLANE)))
    for o in range(1, LAYERS):
        greet(in_layer(lax.rem(layer + o, LAYERS)))
    def remote(src, dst, send, recv, where):
        return pltpu.make_async_remote_copy(
            src_ref=src, dst_ref=dst, send_sem=send, recv_sem=recv, device_id=where,
            device_id_type=MESH,
        )

    two = 2 * W

    def cols(quarter):
        return pl.ds(pl.multiple_of(quarter * W, W), W)

    arrays = (
        (k_hbm, lambda s: kv_own.at[s, :, 0:W]),
        (v_hbm, lambda s: kv_own.at[s, :, W : 2 * W]),
        (q_hbm, lambda s: q_all.at[s]),
        (do_hbm, lambda s: do_all.at[s]),
    )

    def incoming(n, j):
        hbm, place = arrays[n]
        to = lax.rem(part + j, PARTS)
        return remote(
            hbm.at[:, cols(to)], place(part), in_send.at[n, j], in_recv.at[n, j], mate(to)
        )

    def own_copy(n):
        hbm, place = arrays[n]
        return pltpu.make_async_copy(hbm.at[:, cols(part)], place(part), in_recv.at[n, 0])

    def raw_copy(n):
        return pltpu.make_async_copy((k_hbm, v_hbm)[n], kv_raw.at[n], raw_sem.at[n])

    pick_copy = pltpu.make_async_copy(pick_hbm, pick_ref, raw_sem.at[2])
    gid_copy = pltpu.make_async_copy(gid_hbm, gid_ref, raw_sem.at[3])
    gid_copy.start()
    for n in range(2):
        raw_copy(n).start()
    pick_copy.start()
    for n in range(4):
        own_copy(n).start()

    def choose(code, options):
        code = jnp.full((1, options[0].shape[-1]), code, jnp.int32)
        total = None
        for n, option in enumerate(options):
            option = option.astype(F32)
            term = jnp.where(code == n, option, jnp.zeros_like(option))
            total = term if total is None else total + term
        return total.astype(BF)

    def rows(t):
        return pl.ds(pl.multiple_of(t * 16, 16), 16)

    def around(base, count, here, where, source, place):
        def copy(o):
            to = lax.rem(here + o, count)
            return remote(
                source(to), place(here), g_send.at[base, o], g_recv.at[base, o], where(to)
            )
        return copy

    finish = []

    def start_all(copy, count):
        for o in range(1, count):
            copy(o).start()

    def wait_all(copy, count):
        for o in range(1, count):
            copy(o).wait_recv()
        finish.append((copy, count))

    c1 = around(0, PLANE, spot, in_plane, lambda to: cand.at[to], lambda i: g1.at[i])
    c2 = around(1, PARTS, part, mate, lambda to: g2_out.at[to], lambda i: g2.at[i])
    c3 = around(2, LAYERS, layer, in_layer, lambda to: g3.at[layer], lambda i: g3.at[i])
    c4 = around(
        3, PLANE, spot, in_plane, lambda to: kv_glob.at[rows(spot)], lambda i: kv_glob.at[rows(i)]
    )

    to_right = remote(
        kv_own.at[:, BLOCK : 2 * BLOCK, :], kv_left, edge_send.at[0], edge_recv.at[0], right
    )
    to_left = remote(
        kv_own.at[:, 0:BLOCK, :], kv_right, edge_send.at[1], edge_recv.at[1], left
    )

    pl.semaphore_wait(barrier, PARTS - 1 + 2 + PLANE - 1 + LAYERS - 1)


    def send(n, j):
        incoming(n, j).start()

    send(0, 2)
    gid_copy.wait()
    pick_copy.wait()
    my_gid = gid_ref[lax.div(spot, PLANE // GLOBAL)]
    gid_spot = lax.rem(lax.div(my_gid, 2), PLANE)
    gid_layer = lax.rem(lax.div(my_gid, 2 * PLANE), LAYERS)
    gid_part = lax.div(my_gid, 2 * GROUPS)
    for n in range(2):
        raw_copy(n).wait()
    for t in range(PLANE):
        odd = lax.rem(gid_ref[t // (PLANE // GLOBAL)], 2)
        start = (t % (PLANE // GLOBAL)) * 16
        for n in range(2):
            cand[t, :, n * FULL : (n + 1) * FULL] = choose(
                odd, [kv_raw[n, b * BLOCK + start : b * BLOCK + start + 16, :] for b in range(2)]
            )

    start_all(c1, PLANE)
    send(0, 1)
    send(0, 3)
    g1[spot] = cand[spot]
    wait_all(c1, PLANE)
    piece = choose(gid_spot, [g1[t] for t in range(PLANE)])
    for h in range(PARTS):
        g2_out[h, :, 0:W] = piece[:, h * W : (h + 1) * W]
        g2_out[h, :, W:two] = piece[:, FULL + h * W : FULL + (h + 1) * W]
    start_all(c2, PARTS)
    send(1, 2)
    send(1, 1)
    send(1, 3)
    send(2, 2)
    send(3, 2)
    send(2, 1)
    send(3, 1)
    send(2, 3)
    g2[part] = g2_out[part]
    acc_own[...] = jnp.zeros_like(acc_own)
    acc_left[...] = jnp.zeros_like(acc_left)
    acc_right[...] = jnp.zeros_like(acc_right)
    wait_all(c2, PARTS)
    g3[layer] = choose(gid_part, [g2[t] for t in range(PARTS)])
    start_all(c3, LAYERS)
    send(3, 3)

    for n in range(2):
        own_copy(n).wait()
        for j in (1, 3, 2):
            incoming(n, j).wait_recv()
    to_right.start()
    to_left.start()
    wait_all(c3, LAYERS)
    kv_glob[rows(spot), :] = choose(gid_layer, [g3[t] for t in range(LAYERS)])
    start_all(c4, PLANE)
    first_group = (group == 0).astype(jnp.int32)
    last_group = (group == GROUPS - 1).astype(jnp.int32)
    low = lax.broadcasted_iota(jnp.int32, (BLOCK, W), 1) < HALF

    def two_heads(x):
        x = x.astype(F32)
        zero = jnp.zeros_like(x)
        return jnp.concatenate([jnp.where(low, x, zero), jnp.where(low, zero, x)], axis=0)

    def dot(a, b, dims):
        return lax.dot_general(a, b, (dims, ((), ())), preferred_element_type=F32)

    def quarter_of(t):
        j = t + (t == 1).astype(jnp.int32) - (t == 2).astype(jnp.int32)
        return j, lax.rem(part + PARTS - j, PARTS)

    def entries(here, b):
        at_left = lax.rem(here + (PARTS - 1) * first_group, PARTS)
        at_right = lax.rem(here + last_group, PARTS)
        number = here * (2 * GROUPS) + 2 * group + b
        own0 = (kv_own, here, 0, acc_own)
        own1 = (kv_own, here, BLOCK, acc_own)
        window = [
            (kv_left, at_left, 0, acc_left) if b == 0 else own0,
            own0 if b == 0 else own1,
            own1 if b == 0 else (kv_right, at_right, 0, acc_right),
        ]
        choices = []
        for s in range(RAND):
            far = lax.rem(here + PARTS - (s + 1), PARTS)
            far_left = lax.rem(far + (PARTS - 1) * first_group, PARTS)
            pick = jnp.full((1, two), pick_ref[s, number].astype(F32)).astype(BF)
            near_entry = (kv_own, far, b * BLOCK, acc_own)
            far_entry = (kv_left, far_left, 0, acc_left) if b == 0 else (kv_own, far, 0, acc_own)
            choices.append((near_entry, far_entry, pick))
        return number, window, choices

    def load(entry):
        ref, at, start, _ = entry
        return ref[at, start : start + BLOCK, :]

    def add(entry, value):
        _, at, start, acc = entry
        acc[at, start : start + BLOCK, :] += value

    def own_part(t, _):
        j, here = quarter_of(t)
        for n in (2, 3):
            @pl.when(j == 0)
            def _():
                own_copy(n).wait()

            @pl.when(j != 0)
            def _():
                incoming(n, j).wait_recv()

        for b in range(2):
            at = 2 * t + b
            number, window, choices = entries(here, b)
            pieces = [load(e) for e in window]
            for near_entry, far_entry, pick in choices:
                pieces.append(load(near_entry) * (1 - pick) + load(far_entry) * pick)
            listed = jnp.concatenate(pieces, axis=0)
            keys = listed[:, 0:W]
            values = listed[:, W:two]
            q2 = (two_heads(q_all[here, b * BLOCK : (b + 1) * BLOCK, :]) * 0.125).astype(BF)
            do2 = two_heads(do_all[here, b * BLOCK : (b + 1) * BLOCK, :]).astype(BF)
            scores = dot(keys, q2, ((1,), (1,)))
            edge = 0 if b == 0 else 2
            outside = number == (0 if b == 0 else 2 * SEQ - 1)
            masked = jnp.where(outside, -1e30, scores[edge * BLOCK : (edge + 1) * BLOCK])
            ahead = [scores[: edge * BLOCK]] if b else []
            scores = jnp.concatenate(ahead + [masked, scores[(edge + 1) * BLOCK :]], axis=0)
            row_max = jnp.max(scores, axis=0, keepdims=True)
            expo = jnp.exp(scores - row_max)
            keys_near[at] = keys
            q2_all[at] = q2
            do2_all[at] = do2
            expo_near[at] = expo
            gp_near[at] = dot(values, do2, ((1,), (1,)))
            stats[at, 0:1, :] = row_max
            stats[at, 1:2, :] = jnp.sum(expo, axis=0, keepdims=True)
        return 0

    def whole_rows(t, _):
        keys = kv_glob[:, 0:W]
        values = kv_glob[:, W:two]
        for b in range(2):
            at = 2 * t + b
            q2 = q2_all[at]
            do2 = do2_all[at]
            scores = dot(keys, q2, ((1,), (1,)))
            grad_probs = dot(values, do2, ((1,), (1,)))
            near_max = stats[at, 0:1, :]
            row_max = jnp.maximum(near_max, jnp.max(scores, axis=0, keepdims=True))
            shrink = jnp.exp(near_max - row_max)
            expo = jnp.exp(scores - row_max)
            row_total = stats[at, 1:2, :] * shrink + jnp.sum(expo, axis=0, keepdims=True)
            inverse = 1.0 / row_total
            probs = expo * inverse
            probs_half = probs.astype(BF)
            probs_near = expo_near[at] * (shrink * inverse)
            half_near = probs_near.astype(BF)
            gp = gp_near[at]
            row_dot = jnp.sum(probs_half.astype(F32) * grad_probs, axis=0, keepdims=True) + jnp.sum(
                half_near.astype(F32) * gp, axis=0, keepdims=True
            )
            grad_half = (probs * (grad_probs - row_dot)).astype(BF)
            probs_all[at] = half_near
            grads_all[at] = (probs_near * (gp - row_dot)).astype(BF)
            grads_glob[:, cols(at)] = grad_half
            probs_glob[:, cols(at)] = probs_half
        return 0

    def spread(t, _):
        _, here = quarter_of(t)
        for b in range(2):
            at = 2 * t + b
            _, window, choices = entries(here, b)
            grad_near = grads_all[at]
            back = dot(grad_near, keys_near[at], ((0,), (0,))) + dot(
                grads_glob[:, cols(at)], kv_glob[:, 0:W], ((0,), (0,))
            )
            dq_stage[here, b * BLOCK : (b + 1) * BLOCK, :] = (
                jnp.where(low, back[:BLOCK], back[BLOCK:]) * 0.125
            ).astype(BF)
            grads = jnp.concatenate(
                [
                    dot(grad_near, q2_all[at], ((1,), (0,))),
                    dot(probs_all[at], do2_all[at], ((1,), (0,))),
                ],
                axis=1,
            )
            for n, entry in enumerate(window):
                add(entry, grads[n * BLOCK : (n + 1) * BLOCK])
            for n, (near_entry, far_entry, pick) in enumerate(choices):
                part_grad = grads[(3 + n) * BLOCK : (4 + n) * BLOCK]
                far_grad = part_grad * pick.astype(F32)
                add(near_entry, part_grad - far_grad)
                add(far_entry, far_grad)
        return 0

    def outgoing_dq(j):
        to = lax.rem(part + j, PARTS)
        return remote(
            dq_stage.at[to], dq_out.at[:, cols(part)], dq_send.at[j], dq_recv.at[j], mate(to)
        )

    def own_dq():
        return pltpu.make_async_copy(dq_stage.at[part], dq_out.at[:, cols(part)], dq_recv.at[0])

    to_right.wait()
    to_left.wait()
    lax.fori_loop(0, PARTS, own_part, 0)
    wait_all(c4, PLANE)
    lax.fori_loop(0, PARTS, whole_rows, 0, unroll=True)

    d1 = around(4, PLANE, spot, in_plane, lambda to: h1_out.at[to], lambda i: h1.at[i])
    d2 = around(5, LAYERS, layer, in_layer, lambda to: h2.at[layer], lambda i: h2.at[i])
    d3 = around(6, PLANE, spot, in_plane, lambda to: h3.at[spot], lambda i: h3.at[i])

    sums = (
        dot(grads_glob[...], q2_all[...].reshape(2 * PARTS * W, W), ((1,), (0,))),
        dot(probs_glob[...], do2_all[...].reshape(2 * PARTS * W, W), ((1,), (0,))),
    )
    for n in range(2):
        for t in range(PLANE):
            h1_out[t, :, n * W : (n + 1) * W] = sums[n][t * 16 : (t + 1) * 16].astype(BF)
    start_all(d1, PLANE)
    h1[spot] = h1_out[spot]
    lax.fori_loop(0, PARTS, spread, 0)
    own_dq().start()
    wait_all(d1, PLANE)
    h2[layer] = jnp.sum(h1[...].astype(F32), axis=0).astype(BF)
    start_all(d2, LAYERS)
    edge_out[0] = acc_left[...].astype(BF)
    edge_out[1] = acc_right[...].astype(BF)
    back_left = remote(edge_out.at[0], edge_in.at[0], edge_send.at[2], edge_recv.at[2], left)
    back_right = remote(edge_out.at[1], edge_in.at[1], edge_send.at[3], edge_recv.at[3], right)
    back_left.start()
    back_right.start()
    wait_all(d2, LAYERS)
    h3[spot] = jnp.sum(h2[...].astype(F32), axis=0).astype(BF)
    start_all(d3, PLANE)
    outgoing_dq(2).start()
    outgoing_dq(1).start()
    outgoing_dq(3).start()
    back_left.wait()
    back_right.wait()
    for b in range(2):
        acc_own[:, b * BLOCK : (b + 1) * BLOCK, :] += edge_in[1 - b].astype(F32)
    wait_all(d3, PLANE)

    results = ((dk_stage, dk_out), (dv_stage, dv_out))

    def outgoing(n, j):
        stage, out = results[n]
        to = lax.rem(part + j, PARTS)
        return remote(
            stage.at[to], out.at[:, cols(part)], dkv_send.at[n, j], dkv_recv.at[n, j], mate(to)
        )

    def own_out(n):
        stage, out = results[n]
        return pltpu.make_async_copy(stage.at[part], out.at[:, cols(part)], dkv_recv.at[n, 0])

    for j in (2, 1, 3, 0):
        there = lax.rem(part + j, PARTS)
        for b in range(2):
            span = slice(b * BLOCK, (b + 1) * BLOCK)
            number = there * (2 * GROUPS) + 2 * group + b
            total = acc_own[there, span, :]
            for m in range(GLOBAL):
                extra = h3[m * 4 : (m + 1) * 4].reshape(BLOCK, two).astype(F32)
                named = jnp.full((1, two), gid_ref[m], jnp.int32) == number
                total = total + jnp.where(named, extra, jnp.zeros_like(extra))
            dk_stage[there, span, :] = total[:, 0:W].astype(BF)
            dv_stage[there, span, :] = total[:, W:two].astype(BF)
        for n in range(2):
            if j == 0:
                own_out(n).start()
            else:
                outgoing(n, j).start()

    for copy, count in finish:
        for o in range(1, count):
            copy(o).wait_send()
    for n in range(4):
        for j in range(1, PARTS):
            incoming(n, j).wait_send()
    own_dq().wait()
    for j in range(1, PARTS):
        outgoing_dq(j).wait()
    for n in range(2):
        own_out(n).wait()
        for j in range(1, PARTS):
            outgoing(n, j).wait()


def on_device(queries, key_vectors, value_vectors, output_grad, rand_pick, global_ids):
    rows, width = queries.shape
    out = jax.ShapeDtypeStruct((3, rows, width), BF)
    anywhere = pl.BlockSpec(memory_space=pl.ANY)
    two = 2 * W
    scratch = [
        pltpu.VMEM((PARTS, 2 * BLOCK, W), BF),
        pltpu.VMEM((PARTS, 2 * BLOCK, W), BF),
        pltpu.VMEM((PARTS, 2 * BLOCK, two), BF),
        pltpu.VMEM((PARTS, BLOCK, two), BF),
        pltpu.VMEM((PARTS, BLOCK, two), BF),
        pltpu.VMEM((2, 2 * BLOCK, FULL), BF),
        pltpu.VMEM((PLANE, 16, 2 * FULL), BF),
        pltpu.VMEM((PLANE, 16, 2 * FULL), BF),
        pltpu.VMEM((PARTS, 16, two), BF),
        pltpu.VMEM((PARTS, 16, two), BF),
        pltpu.VMEM((LAYERS, 16, two), BF),
        pltpu.VMEM((GLOBAL * BLOCK, two), BF),
        pltpu.VMEM((PARTS, 2 * BLOCK, two), F32),
        pltpu.VMEM((PARTS, BLOCK, two), F32),
        pltpu.VMEM((PARTS, BLOCK, two), F32),
        pltpu.VMEM((2, PARTS, BLOCK, two), BF),
        pltpu.VMEM((2, PARTS, BLOCK, two), BF),
        pltpu.VMEM((PLANE, 16, two), BF),
        pltpu.VMEM((PLANE, 16, two), BF),
        pltpu.VMEM((LAYERS, 16, two), BF),
        pltpu.VMEM((PLANE, 16, two), BF),
        pltpu.VMEM((PARTS, 2 * BLOCK, W), BF),
        pltpu.VMEM((PARTS, 2 * BLOCK, W), BF),
        pltpu.VMEM((PARTS, 2 * BLOCK, W), BF),
        pltpu.VMEM((2 * PARTS, 6 * BLOCK, W), BF),
        pltpu.VMEM((2 * PARTS, 2 * BLOCK, W), BF),
        pltpu.VMEM((2 * PARTS, 2 * BLOCK, W), BF),
        pltpu.VMEM((2 * PARTS, 6 * BLOCK, W), F32),
        pltpu.VMEM((2 * PARTS, 6 * BLOCK, W), F32),
        pltpu.VMEM((2 * PARTS, 8, W), F32),
        pltpu.VMEM((2 * PARTS, 6 * BLOCK, W), BF),
        pltpu.VMEM((2 * PARTS, 6 * BLOCK, W), BF),
        pltpu.VMEM((GLOBAL * BLOCK, 2 * PARTS * W), BF),
        pltpu.VMEM((GLOBAL * BLOCK, 2 * PARTS * W), BF),
        pltpu.SMEM((RAND, 2 * SEQ), jnp.int32),
        pltpu.SMEM((GLOBAL,), jnp.int32),
        pltpu.SemaphoreType.DMA((4,)),
        pltpu.SemaphoreType.DMA((4, PARTS)),
        pltpu.SemaphoreType.DMA((4, PARTS)),
        pltpu.SemaphoreType.DMA((4,)),
        pltpu.SemaphoreType.DMA((4,)),
        pltpu.SemaphoreType.DMA((8, PLANE)),
        pltpu.SemaphoreType.DMA((8, PLANE)),
        pltpu.SemaphoreType.DMA((PARTS,)),
        pltpu.SemaphoreType.DMA((PARTS,)),
        pltpu.SemaphoreType.DMA((2, PARTS)),
        pltpu.SemaphoreType.DMA((2, PARTS)),
    ]
    grads = pl.pallas_call(
        kernel,
        out_shape=out,
        in_specs=[anywhere] * 6,
        out_specs=anywhere,
        scratch_shapes=scratch,
        compiler_params=pltpu.CompilerParams(
            collective_id=1, has_side_effects=True, vmem_limit_bytes=60 * 1024 * 1024
        ),
        name="sparse_attention_grads",
    )(queries, key_vectors, value_vectors, output_grad, rand_pick.T, global_ids)
    return grads[0], grads[1], grads[2]


def solution(mesh):
    spec = P(("doc", "seq"), None)
    return jax.shard_map(
        on_device,
        mesh=mesh,
        in_specs=(spec, spec, spec, spec, P("doc", None), P("doc")),
        out_specs=(spec, spec, spec),
        check_vma=False,
    )
```
